256 devices in a mesh: dp: 32 (over y, z_lo, core), expert: 8 (over x, z_hi).
Axes of the slice: x: 4, y: 4, z: 8 (z_hi: 2, z_lo: 4; z = z_hi * 4 + z_lo), core: 2. Of those that a mesh axis runs over, the one named last changes fastest.
Arguments:
- hidden: bfloat16 [32768, 7168], P('dp', 'expert'), may hold values from -500 to 500
- routes: int32 [32768, 2], P('dp'), may hold values from 0 to 255, all different within a row; in each aligned block of 1024 rows (0 to 1023, 1024 to 2047, ...) at most 10 rows name the same one
- gates: float32 [32768, 2], P('dp'), may hold values from 0.1 to 1
- saved_pre: bfloat16 [32, 320, 2048], P('dp', 'expert'), may hold values from -8 to 8
- w_gate: bfloat16 [32, 7168, 1024], P('dp', 'expert'), may hold values from -0.1875 to 0.1875
- w_up: bfloat16 [32, 7168, 1024], P('dp', 'expert'), may hold values from -0.1875 to 0.1875
- w_down: bfloat16 [32, 1024, 7168], P('dp', None, 'expert'), may hold values from -0.0625 to 0.0625
- mtp_proj: bfloat16 [7168, 3584], P('expert', 'dp'), may hold values from -1 to 1
- mtp_gain: float32 [7168], P('expert'), may hold values from 0.1 to 1.9
- mtp_cotangent: bfloat16 [32768, 3584], P('dp', 'expert'), may hold values from -12 to 12
- main_cotangent: bfloat16 [32768, 7168], P('dp', 'expert'), may hold values from -3 to 3
Outputs:
- grad_input: bfloat16 [32768, 7168], P('dp', 'expert')
- grad_gates: bfloat16 [32768, 2], P('dp')
- grad_proj: float32 [7168, 3584], P('expert', 'dp')
The draws below stay inside these ranges and needn't reach their ends.
Inputs may be any that keep to these rules, and one draw needn't show every extreme that they name: `routes`: ids below 32 are the experts of the window. Among the 1024 tokens of one dp index no id is named more than 10 times.
All inputs are finite; a program needn't handle non-finite values.
Results may differ from the reference program's by a relative error of at most 0.0051.
Values may be sent and summed in bfloat16 or wider, within the bound.
No kernel may reach another device: no remote copies, remote signals or barrier semaphores. Data moves between devices by JAX's collectives and lax.ppermute only.
A program may use at most 128 MiB of HBM per device.

```python
import math
import jax
import jax.numpy as jnp
import numpy as np
from jax import lax

D = 7168
ALL_EXPERTS = 256
FFW = 1024
MOUT = 3584
TOP = 2
TOK_DP = 1024
TOKENS = 32768
EXPERTS = 32
CAP = 10
SLOTS = 320
N_DP = 32


def shared_directions(key):
    feature_key = jax.random.fold_in(key, 301)
    output_key = jax.random.fold_in(key, 302)
    rising = jnp.sqrt(1.0 + 2.0 * jnp.arange(D, dtype=jnp.float32) / D)
    feature_dir = jax.random.normal(feature_key, (D,), jnp.float32) * rising
    output_dir = jax.random.normal(output_key, (MOUT,), jnp.float32)
    return (feature_dir, output_dir)


def token_factor(sign_key, size_key):
    token_sign = jnp.where(jax.random.bernoulli(sign_key, 0.5, (TOKENS, 1)), 1.0, -1.0)
    return token_sign * jax.random.uniform(size_key, (TOKENS, 1), jnp.float32, 0.7, 1.3)


def draw_hidden(key, part):
    feature_dir, output_dir = shared_directions(key)
    key = jax.random.fold_in(key, 11)
    noise_key = jax.random.fold_in(key, 0)
    row_key = jax.random.fold_in(key, 1)
    col_key = jax.random.fold_in(key, 2)
    sign_key = jax.random.fold_in(key, 4)
    size_key = jax.random.fold_in(key, 5)
    row_scale = 10.0 ** jax.random.uniform(row_key, (TOKENS, 1), jnp.float32)
    col_scale = 10.0 ** jax.random.uniform(col_key, (1, D), jnp.float32)
    col_scale = col_scale * jnp.sqrt(1.0 + 2.0 * jnp.arange(D, dtype=jnp.float32)[None, :] / D)
    base = jax.random.normal(noise_key, (TOKENS, D), jnp.float32)
    base = base + token_factor(sign_key, size_key) * feature_dir[None, :]
    return jnp.clip(0.3 * base * row_scale * col_scale, -500.0, 500.0).astype(jnp.bfloat16)


def draw_mtp_proj(key, part):
    feature_dir, output_dir = shared_directions(key)
    key = jax.random.fold_in(key, 13)
    weights = jax.random.normal(key, (D, MOUT), jnp.float32) / jnp.sqrt(jnp.float32(MOUT))
    weights = weights + 1.5 / MOUT * feature_dir[:, None] * output_dir[None, :]
    return jnp.clip(weights, -1.0, 1.0).astype(jnp.bfloat16)


def draw_mtp_cotangent(key, part):
    feature_dir, output_dir = shared_directions(key)
    key = jax.random.fold_in(key, 17)
    noise_key, pair_key, sign_key, size_key = jax.random.split(key, 4)
    noise = jax.random.normal(noise_key, (TOKENS, MOUT), jnp.float32)
    pairing = jax.random.permutation(pair_key, N_DP)
    row_block = jnp.arange(TOKENS, dtype=jnp.int32) // TOK_DP
    col_block = jnp.arange(MOUT, dtype=jnp.int32) // (MOUT // N_DP)
    boosted = pairing[row_block][:, None] == col_block[None, :]
    noise = noise * jnp.where(boosted, 4.0, 1.0)
    values = noise + token_factor(sign_key, size_key) * output_dir[None, :]
    return jnp.clip(values, -12.0, 12.0).astype(jnp.bfloat16)


def block_scale(key, extent, cuts, least, high):
    def one(position, parts):
        steps = jax.random.uniform(jax.random.fold_in(jax.random.fold_in(key, 6), position), (parts,), jnp.float32, least / len(cuts), high / len(cuts))
        return jnp.repeat(jnp.exp(steps), extent[position] // parts).reshape((-1,) + (1,) * (len(extent) - position - 1))

    gain = one(*cuts[0])
    for cut in cuts[1:]:
        gain = gain * one(*cut)
    return gain


def deal_out(rng, own, number, rows, number_of, top, most, slope):
    sequence = jax.random.permutation(rng, number_of)
    crowded, ordinary = load_shares(number_of, rows * top, most, slope, True), load_shares(number_of, rows * top, most, slope, False)
    places = jnp.arange(number_of)

    def named(lengths, rotation):
        used = int((lengths > 0).sum())
        fixed = max(1, used // 4)
        shifted = fixed + (places - fixed + rotation * (used - fixed)) % max(1, number_of - fixed)
        return jnp.zeros((number_of,), jnp.int32).at[sequence[jnp.where(places < fixed, places, shifted)]].set(jnp.asarray(lengths, jnp.int32))

    lengths = jnp.where(number % 4 == 0, named(crowded, number // 4), named(ordinary, number - number // 4 - 1))
    mixed = jax.random.permutation(jax.random.fold_in(own, 3), number_of)
    giver, taker = mixed[0:number_of // 2 * 2:2], mixed[1:number_of // 2 * 2:2]
    margin = jnp.minimum(lengths[giver] - 1, most - lengths[taker]) // 2
    margin = jnp.where((giver == sequence[0]) | (taker == sequence[0]) | (lengths[taker] == 0), 0, jnp.maximum(margin, 0))
    shifted = jax.random.randint(jax.random.fold_in(own, 4), (number_of // 2,), 0, 1 << 20) % (margin + 1)
    lengths = lengths.at[giver].add(-shifted).at[taker].add(shifted)
    items = jnp.searchsorted(jnp.cumsum(lengths), jnp.arange(rows * top), side="right").astype(jnp.int32)
    grid = items.reshape(top, rows).T
    grid = grid[jax.random.permutation(jax.random.fold_in(own, 1), rows)]
    rotation = jax.random.randint(jax.random.fold_in(own, 2), (rows, 1), 0, top)
    return jnp.take_along_axis(grid, (jnp.arange(top)[None, :] + rotation) % top, axis=1)


def load_shares(number_of, total, most, lean, full):
    portions = [(1 << 20) // math.isqrt(grade ** lean) + 1 for grade in range(1, number_of + 1)]
    largest = most if full else min(most, max(-(-total // number_of), total * portions[0] // sum(portions)))
    least = 1 if total - largest >= number_of - 1 else 0
    counts, spare = [largest] + [least] * (number_of - 1), total - largest - least * (number_of - 1)
    while spare > 0:
        movable = [i for i in range(1, number_of) if counts[i] < largest] or [i for i in range(1, number_of) if counts[i] < most]
        whole, budget = sum([portions[i] for i in movable]), spare
        for i in movable:
            addition = min(most - counts[i], max(1, budget * portions[i] // whole), spare)
            counts[i] = counts[i] + addition
            spare = spare - addition
    return np.array(counts)


def gaussian(own_key, extent, deviation, reach, cuts=(), kind=jnp.bfloat16):
    drawn = jax.random.normal(own_key, extent, jnp.float32) * deviation
    if len(cuts) > 0:
        drawn = block_scale(own_key, extent, cuts, -0.22, 0.18) * drawn
    return jnp.clip(drawn, min=-reach, max=reach).astype(kind)


def setup_inputs(seed: int = 0) -> dict:
    seeds = jax.random.split(jax.random.key(seed), 12)
    hidden = draw_hidden(jax.random.fold_in(seeds[11], 71), 0)
    routes_keys = jax.random.split(jax.random.fold_in(seeds[1], 1), TOKENS // TOK_DP)
    routes_turns = jax.random.permutation(jax.random.fold_in(seeds[1], 3), TOKENS // TOK_DP)
    routes = jax.vmap(lambda own, number: deal_out(jax.random.fold_in(seeds[1], 2), own, number, TOK_DP, ALL_EXPERTS, TOP, CAP, 1))(routes_keys, routes_turns).reshape((TOKENS, TOP))
    gates = jnp.clip(0.1 + 0.9 * jax.random.uniform(seeds[2], (TOKENS, TOP), jnp.float32) ** block_scale(seeds[2], (TOKENS, TOP), ((0, 32),), -0.2, 0.2), 0.1, 1.0)
    saved_pre = gaussian(seeds[3], (EXPERTS, SLOTS, 2 * FFW), 1.5, 8.0, ((0, 32), (1, 8)))
    w_gate = gaussian(seeds[4], (EXPERTS, D, FFW), FFW ** -0.5, 0.1875, ((0, 32), (1, 8)))
    w_up = gaussian(seeds[5], (EXPERTS, D, FFW), FFW ** -0.5, 0.1875, ((0, 32), (1, 8)))
    w_down = gaussian(seeds[6], (EXPERTS, FFW, D), D ** -0.5, 0.0625, ((0, 32), (2, 8)))
    mtp_proj = draw_mtp_proj(jax.random.fold_in(seeds[11], 71), 0)
    mtp_gain = jnp.clip(1.0 + 0.18 * jax.random.normal(seeds[8], (D,), jnp.float32), 0.1, 1.9)
    mtp_cotangent = draw_mtp_cotangent(jax.random.fold_in(seeds[11], 71), 0)
    main_cotangent = gaussian(seeds[10], (TOKENS, D), 0.3, 3.0, ((0, 32), (1, 8)))
    return dict(hidden=hidden, routes=routes, gates=gates, saved_pre=saved_pre, w_gate=w_gate, w_up=w_up, w_down=w_down, mtp_proj=mtp_proj, mtp_gain=mtp_gain, mtp_cotangent=mtp_cotangent, main_cotangent=main_cotangent)


eps = 1e-06

def route_slots(routes, experts, capacity):
    flat = routes.reshape(-1).astype(jnp.int32)
    inside = flat < experts
    onehot = ((flat[:, None] == jnp.arange(experts, dtype=jnp.int32)[None, :]) & inside[:, None]).astype(jnp.int32)
    ranks = jnp.cumsum(onehot, axis=0) - 1
    slot = lax.optimization_barrier(jnp.sum(ranks * onehot, axis=1)).astype(jnp.int32)
    target = jnp.where(inside, flat * capacity + slot, 0).astype(jnp.int32)
    return (flat, inside, target)

def unit_step(pre, summed, units):
    gate = pre[:, :units].astype(jnp.float32)
    upper = pre[:, units:].astype(jnp.float32)
    sig = jax.nn.sigmoid(gate)
    share = lax.optimization_barrier(jnp.sum(gate * sig * upper * summed, axis=1))
    dgate = summed * upper * sig * (1.0 + gate * (1.0 - sig))
    dupper = summed * gate * sig
    both = jnp.concatenate([dgate, dupper], axis=1).astype(jnp.bfloat16)
    return (both, share.astype(jnp.bfloat16))

def reference(hidden, routes, gates, saved_pre, w_gate, w_up, w_down, mtp_proj, mtp_gain, mtp_cotangent, main_cotangent):
    blocks = (hidden.reshape(N_DP, TOK_DP, D), routes.reshape(N_DP, TOK_DP, TOP), mtp_cotangent.reshape(N_DP, TOK_DP, MOUT), main_cotangent.reshape(N_DP, TOK_DP, D))

    def front(carry, block):
        h_blk, r_blk, g_blk, m_blk = block
        hf = h_blk.astype(jnp.float32)
        inverse = lax.rsqrt(lax.optimization_barrier(jnp.sum(hf * hf, axis=1)) / D + eps)
        normed = (hf * inverse[:, None] * mtp_gain[None, :]).astype(jnp.bfloat16)
        normed_grad = jnp.dot(g_blk, mtp_proj.T, preferred_element_type=jnp.float32)
        term = jnp.dot(normed.T, g_blk, preferred_element_type=jnp.float32)
        inner = lax.optimization_barrier(jnp.sum(hf * mtp_gain[None, :] * normed_grad, axis=1))
        hidden_grad = m_blk.astype(jnp.float32) + inverse[:, None] * mtp_gain[None, :] * normed_grad - hf * (inverse ** 3 * inner / D)[:, None]
        sent = hidden_grad.astype(jnp.bfloat16)
        flat, inside, target = route_slots(r_blk, N_DP, CAP)
        index = jnp.where(inside, target, N_DP * CAP).astype(jnp.int32)
        buffer = jnp.zeros((N_DP * CAP + 1, D), jnp.bfloat16).at[index].set(jnp.repeat(sent, TOP, axis=0))
        return (carry + term, (hidden_grad, buffer[:-1].reshape(N_DP, CAP, D)))
    grad_proj, (hidden_grads, buffers) = lax.scan(front, jnp.zeros((D, MOUT), jnp.float32), blocks)
    per_expert = buffers.transpose(1, 0, 2, 3).reshape(N_DP, N_DP * CAP, D)

    def expert(args):
        rows, pre, wg, wu, wd = args
        summed = jnp.dot(rows, wd.T, preferred_element_type=jnp.float32)
        both, share = unit_step(pre, summed, FFW)
        back = (jnp.dot(both[:, :FFW], wg.T, preferred_element_type=jnp.float32) + jnp.dot(both[:, FFW:], wu.T, preferred_element_type=jnp.float32)).astype(jnp.bfloat16)
        return (back, share)
    backs, shares = lax.map(expert, (per_expert, saved_pre, w_gate, w_up, w_down))
    backs = backs.reshape(N_DP, N_DP, CAP, D).transpose(1, 0, 2, 3)
    shares = shares.reshape(N_DP, N_DP, CAP).transpose(1, 0, 2)

    def finish(block):
        hg, r_blk, gate_blk, back_blk, share_blk = block
        flat, inside, target = route_slots(r_blk, N_DP, CAP)
        rows_back = back_blk.reshape(-1, D)[target].astype(jnp.float32)
        scale = jnp.where(inside, gate_blk.reshape(-1), 0.0)
        added = (rows_back * scale[:, None]).reshape(TOK_DP, TOP, D).sum(axis=1)
        grad_input = (hg + added).astype(jnp.bfloat16)
        grad_gate = jnp.where(inside, share_blk.reshape(-1)[target], jnp.zeros((), jnp.bfloat16))
        return (grad_input, grad_gate.reshape(TOK_DP, TOP).astype(jnp.bfloat16))
    grad_input, grad_gates = lax.map(finish, (hidden_grads, routes.reshape(N_DP, TOK_DP, TOP), gates.reshape(N_DP, TOK_DP, TOP), backs, shares))
    return (grad_input.reshape(TOKENS, D), grad_gates.reshape(TOKENS, TOP), grad_proj)
```

```python
import jax
import jax.numpy as jnp
from jax import lax
from jax.experimental import pallas as pl
from jax.experimental.pallas import tpu as pltpu
from jax.sharding import PartitionSpec as P

D = 7168
EPS = 1e-06
NX, NZH = 4, 2
NY, NZ, NC = 4, 4, 2
NE = NX * NZH
BF = jnp.bfloat16
F32 = jnp.float32


def expert_move(value, dx, dz):
    pairs = [
        (x * NZH + h, ((x + dx) % NX) * NZH + (h + dz) % NZH) for x in range(NX) for h in range(NZH)
    ]
    return lax.ppermute(value, "expert", pairs)


def dp_move(value, dy, dz, dc):
    pairs = [
        ((y * NZ + z) * NC + c, (((y + dy) % NY) * NZ + (z + dz) % NZ) * NC + (c + dc) % NC)
        for y in range(NY)
        for z in range(NZ)
        for c in range(NC)
    ]
    return lax.ppermute(value, "dp", pairs)


def expert_sum(value):
    value = value + expert_move(value, 0, 1)
    return (
        (value + expert_move(value, 1, 0))
        + (expert_move(value, 2, 0) + expert_move(value, 3, 0))
    )


def block_of(array, index):
    return lax.dynamic_index_in_dim(array, index, 0, keepdims=False)


def ring_x(block):
    half = block.shape[0] // 2
    below = expert_move(block, 1, 0)
    above = expert_move(block, 3, 0)
    first = expert_move(below[:half], 1, 0)
    second = expert_move(above[half:], 3, 0)
    return below, above, first, second


def gather_expert(block):
    me = lax.axis_index("expert")
    x, h = me // NZH, me % NZH
    rows, cols = block.shape
    half = rows // 2
    out = jnp.zeros((NE, rows, cols), block.dtype)

    def put(out, piece, dx, z, row):
        at = ((x + dx) % NX) * NZH + z
        return lax.dynamic_update_slice(out, piece[None], (at, row, 0))

    def spread(out, piece, z, row):
        n = piece.shape[0] // 2
        below, above, first, second = ring_x(piece)
        out = put(out, piece, 0, z, row)
        out = put(out, below, 3, z, row)
        out = put(out, above, 1, z, row)
        out = put(out, first, 2, z, row)
        return put(out, second, 2, z, row + n)

    top = expert_move(block[:half], 0, 1)
    bottom = expert_move(block[half:], 0, 1)
    out = spread(out, block, h, 0)
    out = spread(out, top, 1 - h, 0)
    return spread(out, bottom, 1 - h, half)


def grad_kernel(cot_ref, proj_ref, hidden_ref, gain_ref, ng_ref, inner_ref):
    acc = jnp.zeros(ng_ref.shape, F32)
    for k in range(NE):
        acc = acc + jnp.dot(cot_ref[k], proj_ref[k], preferred_element_type=F32)
    ng_ref[...] = acc
    weighted = hidden_ref[...].astype(F32) * gain_ref[...] * acc
    total = jnp.sum(weighted, axis=1, keepdims=True)
    inner_ref[...] = jnp.broadcast_to(total, inner_ref.shape)


def normed_grad_of(cot, proj, hidden, gain):
    tokens, feats = hidden.shape
    width = cot.shape[2]
    tile = 256
    return pl.pallas_call(
        grad_kernel,
        grid=(tokens // tile,),
        in_specs=[
            pl.BlockSpec((NE, tile, width), lambda i: (0, i, 0)),
            pl.BlockSpec((NE, width, feats), lambda i: (0, 0, 0)),
            pl.BlockSpec((tile, feats), lambda i: (i, 0)),
            pl.BlockSpec((1, feats), lambda i: (0, 0)),
        ],
        out_specs=[
            pl.BlockSpec((tile, feats), lambda i: (i, 0)),
            pl.BlockSpec((tile, 128), lambda i: (i, 0)),
        ],
        out_shape=[
            jax.ShapeDtypeStruct((tokens, feats), F32),
            jax.ShapeDtypeStruct((tokens, 128), F32),
        ],
        cost_estimate=pl.CostEstimate(
            flops=2 * tokens * feats * NE * width, bytes_accessed=20_000_000, transcendentals=0
        ),
        compiler_params=pltpu.CompilerParams(vmem_limit_bytes=48 * 2**20),
        name="normed_grad",
    )(cot, proj, hidden, gain)


def proj_kernel(core_ref, cot_ref, normed_ref, own_ref, other_ref):
    acc = lax.dot_general(
        cot_ref[0], normed_ref[...], (((0,), (0,)), ((), ())), preferred_element_type=F32
    )
    size = own_ref.shape[2]
    first = core_ref[0] == 0
    for z in range(2):
        zero = acc[(2 * z) * size : (2 * z + 1) * size]
        one = acc[(2 * z + 1) * size : (2 * z + 2) * size]
        own_ref[0, z] = jnp.where(first, zero, one)
        other_ref[0, z] = jnp.where(first, one, zero).astype(BF)


def proj_partials(cot, normed, core):
    tokens, feats = normed.shape
    width = cot.shape[2]
    size = width // 4
    return pl.pallas_call(
        proj_kernel,
        grid_spec=pltpu.PrefetchScalarGridSpec(
            num_scalar_prefetch=1,
            grid=(NE,),
            in_specs=[
                pl.BlockSpec((1, tokens, width), lambda i, c: (i, 0, 0)),
                pl.BlockSpec((tokens, feats), lambda i, c: (0, 0)),
            ],
            out_specs=[
                pl.BlockSpec((1, 2, size, feats), lambda i, c: (i, 0, 0, 0)),
                pl.BlockSpec((1, 2, size, feats), lambda i, c: (i, 0, 0, 0)),
            ],
        ),
        out_shape=[
            jax.ShapeDtypeStruct((NE, 2, size, feats), F32),
            jax.ShapeDtypeStruct((NE, 2, size, feats), BF),
        ],
        cost_estimate=pl.CostEstimate(
            flops=2 * tokens * feats * NE * width, bytes_accessed=20_000_000, transcendentals=0
        ),
        compiler_params=pltpu.CompilerParams(vmem_limit_bytes=48 * 2**20),
        name="proj_partials",
    )(core.reshape(1), cot, normed)


def scatter_proj(own, other):
    me = lax.axis_index("dp")
    y, z = me // (NZ * NC), (me // NC) % NZ
    size, feats = own.shape[2:]
    own = own.reshape(NY, NZ, size, feats)
    got = dp_move(other, 0, 0, 1).reshape(NY, NZ, size, feats)

    def chip(dy):
        at = (y + dy) % NY
        return block_of(own, at) + block_of(got, at).astype(F32)

    moved = [dp_move(chip(d).astype(BF), d, 0, 0) for d in (1, 3, 2)]
    line = chip(0) + moved[0].astype(F32) + moved[1].astype(F32) + moved[2].astype(F32)
    sent = line.astype(BF)
    moved = [dp_move(block_of(sent, (z + d) % NZ), 0, d, 0) for d in (1, 3, 2)]
    total = block_of(line, z) + moved[0].astype(F32) + moved[1].astype(F32) + moved[2].astype(F32)
    return total.T


def against(left, right):
    return lax.dot_general(left, right, (((1,), (1,)), ((), ())), preferred_element_type=F32)


def unit_step(pre, summed, units):
    gate = pre[:, :units].astype(F32)
    upper = pre[:, units:].astype(F32)
    sig = jax.nn.sigmoid(gate)
    share = jnp.sum(gate * sig * upper * summed, axis=1)
    dgate = summed * upper * sig * (1.0 + gate * (1.0 - sig))
    dupper = summed * gate * sig
    return dgate.astype(BF), dupper.astype(BF), share.astype(BF)


def slot_tables(routes, gates, experts, capacity):
    tokens = routes.shape[0]
    ids = jnp.arange(experts, dtype=jnp.int32)[:, None]
    first, second = routes[:, 0][None, :] == ids, routes[:, 1][None, :] == ids
    named = first | second
    before = (
        lax.broadcasted_iota(jnp.int32, (tokens, tokens), 0)
        < lax.broadcasted_iota(jnp.int32, (tokens, tokens), 1)
    ).astype(BF)
    ranks = jnp.dot(named.astype(BF), before, preferred_element_type=F32)
    place = jnp.where(named, ranks + 1.0, 0.0).astype(BF)
    slots = experts * capacity
    row = lax.broadcasted_iota(jnp.int32, (slots, experts), 0)
    spread = (row // capacity == lax.broadcasted_iota(jnp.int32, (slots, experts), 1)).astype(BF)
    want = (jnp.arange(slots, dtype=jnp.int32) % capacity + 1).astype(F32)
    chosen = jnp.dot(spread, place, preferred_element_type=F32) == want[:, None]
    gate = jnp.where(first, gates[:, 0][None, :], jnp.where(second, gates[:, 1][None, :], 0.0))
    weight = jnp.dot(
        spread.astype(F32), gate, precision=lax.Precision.HIGHEST, preferred_element_type=F32
    )
    weight = jnp.where(chosen, weight, 0.0)
    high = weight.astype(BF)
    low = (weight - high.astype(F32)).astype(BF)
    return chosen.astype(BF), high, low, spread, first, second


def over_slots(table, rows):
    return lax.dot_general(table, rows, (((0,), (0,)), ((), ())), preferred_element_type=F32)


def sum_expert_rows(partial):
    me = lax.axis_index("expert")
    x = me // NZH
    slots, units = partial.shape
    blocks = partial.reshape(NX, slots // NX, units)
    moved = [expert_move(block_of(blocks, (x + d) % NX).astype(BF), d, 0) for d in (1, 3, 2)]
    mine = block_of(blocks, x)
    mine = ((mine + moved[0].astype(F32)) + (moved[1].astype(F32) + moved[2].astype(F32))).astype(BF)
    swapped = expert_move(mine, 0, 1)
    mine = (mine.astype(F32) + swapped.astype(F32)).astype(BF)
    out = jnp.zeros((NX, slots // NX, units), BF)

    def put(out, piece, dx):
        return lax.dynamic_update_slice(out, piece[None], ((x + dx) % NX, 0, 0))

    out = put(out, mine, 0)
    for d in (1, 3, 2):
        out = put(out, expert_move(mine, d, 0), NX - d)
    return out.reshape(slots, units)


def per_device(
    hidden,
    routes,
    gates,
    saved_pre,
    w_gate,
    w_up,
    w_down,
    mtp_proj,
    mtp_gain,
    mtp_cotangent,
    main_cotangent,
):
    tokens, feats = hidden.shape
    experts = lax.axis_size("dp")
    slots = saved_pre.shape[1] * NE
    capacity = slots // experts
    units = w_down.shape[1]
    core = lax.axis_index("dp") % NC

    proj = lax.all_gather(mtp_proj.T, "dp", axis=0, tiled=True)
    proj = proj.reshape(NE, mtp_cotangent.shape[1], feats)
    pre = lax.all_gather(saved_pre[0], "expert", axis=0, tiled=True)
    cot = gather_expert(mtp_cotangent)

    hidden_f = hidden.astype(F32)
    gain = mtp_gain[None, :]
    squares = expert_sum(jnp.sum(hidden_f * hidden_f, axis=1).reshape(8, tokens // 8))
    inverse = lax.rsqrt(squares.reshape(tokens) / D + EPS)
    normed = (hidden_f * inverse[:, None] * gain).astype(BF)
    chosen, high, low, spread, first, second = slot_tables(routes, gates, experts, capacity)

    normed_grad, inner = normed_grad_of(cot, proj, hidden, gain)
    inner = expert_sum(inner[:, 0].reshape(8, tokens // 8)).reshape(tokens)
    hidden_grad = (
        main_cotangent.astype(F32)
        + inverse[:, None] * gain * normed_grad
        - hidden_f * (inverse**3 * inner / D)[:, None]
    )
    sent = hidden_grad.astype(BF)
    outgoing = jnp.dot(chosen, sent, preferred_element_type=F32).astype(BF)
    arrived = lax.all_to_all(
        outgoing.reshape(experts, capacity, feats), "dp", split_axis=0, concat_axis=0, tiled=True
    ).reshape(slots, feats)

    own, other = proj_partials(cot, normed, core)
    grad_proj = scatter_proj(own, other)

    summed = sum_expert_rows(against(arrived, w_down[0])).astype(F32)
    dgate, dupper, share = unit_step(pre, summed, units)
    back = (against(dgate, w_gate[0]) + against(dupper, w_up[0])).astype(BF)
    returned = lax.all_to_all(
        back.reshape(experts, capacity, feats), "dp", split_axis=0, concat_axis=0, tiled=True
    ).reshape(slots, feats)
    returned_share = lax.all_to_all(
        share.reshape(experts, capacity), "dp", split_axis=0, concat_axis=0, tiled=True
    ).reshape(slots)

    added = over_slots(high, returned) + over_slots(low, returned)
    grad_input = (hidden_grad + added).astype(BF)
    by_expert = lax.dot_general(
        spread * returned_share[:, None], chosen, (((0,), (0,)), ((), ())), preferred_element_type=F32
    )
    grad_gates = jnp.stack(
        [
            jnp.sum(jnp.where(first, by_expert, 0.0), axis=0),
            jnp.sum(jnp.where(second, by_expert, 0.0), axis=0),
        ],
        axis=1,
    ).astype(BF)
    return (grad_input, grad_gates, grad_proj)


def solution(mesh):
    return jax.shard_map(
        per_device,
        mesh=mesh,
        in_specs=(
            P("dp", "expert"),
            P("dp", None),
            P("dp", None),
            P("dp", "expert", None),
            P("dp", "expert", None),
            P("dp", "expert", None),
            P("dp", None, "expert"),
            P("expert", "dp"),
            P("expert"),
            P("dp", "expert"),
            P("dp", "expert"),
        ),
        out_specs=(P("dp", "expert"), P("dp", None), P("expert", "dp")),
        check_vma=False,
    )
```

```python
import jax
import jax.numpy as jnp
from jax import lax
from jax.experimental import pallas as pl
from jax.experimental.pallas import tpu as pltpu
from jax.sharding import PartitionSpec as P

D = 7168
EPS = 1e-06
NX, NZH = 4, 2
NY, NZ, NC = 4, 4, 2
NE = NX * NZH
ND = NY * NZ * NC
BF = jnp.bfloat16
F32 = jnp.float32
STEPS = (1, 3, 2)
PIECES = tuple((d, h) for h in (0, 1) for d in (0,) + STEPS)
ANY = pl.BlockSpec(memory_space=pl.ANY)
VM = pl.BlockSpec(memory_space=pltpu.VMEM)
SM = pl.BlockSpec(memory_space=pltpu.SMEM)
VMEM_BYTES = 48 * 2**20


def expert_move(value, dx, dz):
    pairs = [
        (x * NZH + h, ((x + dx) % NX) * NZH + (h + dz) % NZH) for x in range(NX) for h in range(NZH)
    ]
    return lax.ppermute(value, "expert", pairs)


def dp_move(value, dy, dz, dc):
    pairs = [
        ((y * NZ + z) * NC + c, (((y + dy) % NY) * NZ + (z + dz) % NZ) * NC + (c + dc) % NC)
        for y in range(NY)
        for z in range(NZ)
        for c in range(NC)
    ]
    return lax.ppermute(value, "dp", pairs)


def expert_sum(value):
    value = value + expert_move(value, 0, 1)
    return (value + expert_move(value, 1, 0)) + (expert_move(value, 2, 0) + expert_move(value, 3, 0))


def block_of(array, index):
    return lax.dynamic_index_in_dim(array, index, 0, keepdims=False)


def expert_pieces(block):
    swapped = expert_move(block, 0, 1)
    out = [block] + [expert_move(block, d, 0) for d in STEPS]
    return out + [swapped] + [expert_move(swapped, d, 0) for d in STEPS]


def gather_proj(shard):
    line = [dp_move(shard, 0, d, 0) for d in STEPS]
    near = [(shard, [(0, 0, 0)])]
    near += [(dp_move(shard, d, 0, 0), [(d, 0, 0)]) for d in STEPS]
    stack = jnp.concatenate(line, axis=0)
    near += [(stack, [(0, e, 0) for e in STEPS])]
    near += [(dp_move(stack, d, 0, 0), [(d, e, 0) for e in STEPS]) for d in STEPS]
    far = [(dp_move(a, 0, 0, 1), [(y, z, 1) for y, z, _ in steps]) for a, steps in near]
    return near + far


def proj_copies(scalars, refs, layout, scratch, sems, size):
    y, z, c = scalars[0], scalars[1], scalars[2]
    copies = []
    for ref, steps in zip(refs, layout):
        for i, (dy, dz, dc) in enumerate(steps):
            at = ((y + NY - dy) % NY * NZ + (z + NZ - dz) % NZ) * NC + (c + dc) % NC
            row = pl.multiple_of(at * size, 16)
            copies.append(
                pltpu.make_async_copy(
                    ref.at[pl.ds(i * size, size)], scratch.at[pl.ds(row, size)], sems.at[len(copies)]
                )
            )
    return copies


def first_kernel(layout, scalars, *refs):
    n = len(layout)
    proj_refs, cot_refs = refs[:n], refs[n : n + NE]
    hidden_ref, gain_ref, ng_ref, inner_ref, proj, cot, proj_sems, cot_sems = refs[n + NE :]
    rows, width = cot_refs[0].shape
    copies = proj_copies(scalars, proj_refs, layout, proj, proj_sems, width // 4)
    cot_copies = [pltpu.make_async_copy(cot_refs[k], cot.at[k], cot_sems.at[k]) for k in range(NE)]
    for copy in copies + cot_copies:
        copy.start()
    for copy in copies + cot_copies:
        copy.wait()
    acc = jnp.zeros(ng_ref.shape, F32)
    for k in range(NE):
        row = pl.multiple_of(scalars[8 + k] * width, 64)
        acc = acc + jnp.dot(cot[k], proj[pl.ds(row, width), :], preferred_element_type=F32)
    ng_ref[...] = acc
    total = jnp.sum(hidden_ref[...].astype(F32) * gain_ref[...] * acc, axis=1, keepdims=True)
    inner_ref[...] = jnp.broadcast_to(total, inner_ref.shape)


def first_grads(scalars, proj, cots, hidden, gain):
    rows, width = cots[0].shape
    feats = hidden.shape[1]
    layout = [steps for _, steps in proj]
    return pl.pallas_call(
        lambda *refs: first_kernel(layout, *refs),
        grid=(1,),
        in_specs=[SM]
        + [ANY] * (len(proj) + NE)
        + [pl.BlockSpec((rows, feats), lambda i: (0, 0)), pl.BlockSpec((1, feats), lambda i: (0, 0))],
        out_specs=[
            pl.BlockSpec((rows, feats), lambda i: (0, 0)),
            pl.BlockSpec((rows, 128), lambda i: (0, 0)),
        ],
        out_shape=[
            jax.ShapeDtypeStruct((rows, feats), F32),
            jax.ShapeDtypeStruct((rows, 128), F32),
        ],
        scratch_shapes=[
            pltpu.VMEM((NE * width, feats), BF),
            pltpu.VMEM((NE, rows, width), BF),
            pltpu.SemaphoreType.DMA((ND,)),
            pltpu.SemaphoreType.DMA((NE,)),
        ],
        cost_estimate=pl.CostEstimate(
            flops=2 * rows * feats * NE * width, bytes_accessed=12_000_000, transcendentals=0
        ),
        compiler_params=pltpu.CompilerParams(vmem_limit_bytes=VMEM_BYTES),
        name="first_grads",
    )(scalars, *[a for a, _ in proj], *cots, hidden, gain)


def rest_kernel(layout, lead, scalars, *refs):
    n = len(layout)
    proj_refs, lead_refs, cot_refs = refs[:n], refs[n : n + NE], refs[n + NE : n + 2 * NE]
    hidden_ref, gain_ref, normed_ref, ng_ref, inner_ref, own_ref, other_ref = refs[
        n + 2 * NE : n + 2 * NE + 7
    ]
    proj, cot, acc, proj_sems, lead_sems, cot_sems = refs[n + 2 * NE + 7 :]
    width = cot.shape[2]
    rest = cot.shape[1] - lead
    size = width // 4
    step = pl.program_id(0)

    @pl.when(step == 0)
    def _():
        copies = proj_copies(scalars, proj_refs, layout, proj, proj_sems, size)
        for k in range(NE):
            copies.append(
                pltpu.make_async_copy(lead_refs[k], cot.at[k, pl.ds(0, lead)], lead_sems.at[k])
            )
            copies.append(
                pltpu.make_async_copy(cot_refs[k], cot.at[k, pl.ds(lead, rest)], cot_sems.at[k])
            )
        for copy in copies:
            copy.start()
        for copy in copies:
            copy.wait()
        acc[...] = jnp.zeros(acc.shape, F32)

    part = lax.dot_general(
        cot[step], normed_ref[...], (((0,), (0,)), ((), ())), preferred_element_type=F32
    )
    first = scalars[2] == 0
    for z in range(2):
        zero = part[(2 * z) * size : (2 * z + 1) * size]
        one = part[(2 * z + 1) * size : (2 * z + 2) * size]
        own_ref[0, z] = jnp.where(first, zero, one)
        other_ref[0, z] = jnp.where(first, one, zero).astype(BF)
    row = pl.multiple_of(scalars[8 + step] * width, 64)
    acc[...] += jnp.dot(
        cot[step, lead:, :], proj[pl.ds(row, width), :], preferred_element_type=F32
    )

    @pl.when(step == NE - 1)
    def _():
        ng_ref[...] = acc[...]
        weighted = hidden_ref[lead:, :].astype(F32) * gain_ref[...] * acc[...]
        inner_ref[...] = jnp.broadcast_to(
            jnp.sum(weighted, axis=1, keepdims=True), inner_ref.shape
        )


def rest_grads(scalars, proj, leads, cots, hidden, gain, normed):
    lead, width = leads[0].shape
    rest = cots[0].shape[0]
    tokens, feats = hidden.shape
    size = width // 4
    layout = [steps for _, steps in proj]
    whole = lambda *shape: pl.BlockSpec(shape, lambda i, s: (0,) * len(shape))
    placed = pl.BlockSpec((1, 2, size, feats), lambda i, s: (s[8 + i], 0, 0, 0))
    return pl.pallas_call(
        lambda *refs: rest_kernel(layout, lead, *refs),
        grid_spec=pltpu.PrefetchScalarGridSpec(
            num_scalar_prefetch=1,
            grid=(NE,),
            in_specs=[ANY] * (len(proj) + 2 * NE)
            + [whole(tokens, feats), whole(1, feats), whole(tokens, feats)],
            out_specs=[whole(rest, feats), whole(rest, 128), placed, placed],
            scratch_shapes=[
                pltpu.VMEM((NE * width, feats), BF),
                pltpu.VMEM((NE, tokens, width), BF),
                pltpu.VMEM((rest, feats), F32),
                pltpu.SemaphoreType.DMA((ND,)),
                pltpu.SemaphoreType.DMA((NE,)),
                pltpu.SemaphoreType.DMA((NE,)),
            ],
        ),
        out_shape=[
            jax.ShapeDtypeStruct((rest, feats), F32),
            jax.ShapeDtypeStruct((rest, 128), F32),
            jax.ShapeDtypeStruct((NE, 2, size, feats), F32),
            jax.ShapeDtypeStruct((NE, 2, size, feats), BF),
        ],
        cost_estimate=pl.CostEstimate(
            flops=2 * (tokens + rest) * feats * NE * width,
            bytes_accessed=40_000_000,
            transcendentals=0,
        ),
        compiler_params=pltpu.CompilerParams(vmem_limit_bytes=VMEM_BYTES),
        name="rest_grads",
    )(scalars, *[a for a, _ in proj], *leads, *cots, hidden, gain, normed)


def scatter_proj(own, other):
    me = lax.axis_index("dp")
    y, z = me // (NZ * NC), (me // NC) % NZ
    size, feats = own.shape[2:]
    own = own.reshape(NY, NZ, size, feats)
    got = dp_move(other, 0, 0, 1).reshape(NY, NZ, size, feats)

    def chip(dy):
        at = (y + dy) % NY
        return block_of(own, at) + block_of(got, at).astype(F32)

    moved = [dp_move(chip(d).astype(BF), d, 0, 0) for d in STEPS]
    line = chip(0) + moved[0].astype(F32) + moved[1].astype(F32) + moved[2].astype(F32)
    sent = line.astype(BF)
    moved = [dp_move(block_of(sent, (z + d) % NZ), 0, d, 0) for d in STEPS]
    total = block_of(line, z) + moved[0].astype(F32) + moved[1].astype(F32) + moved[2].astype(F32)
    return total.T


NT = (((1,), (1,)), ((), ()))


def dispatch_kernel(ng, hidden, main, gain, scale, pull, chosen, grad_ref, out_ref):
    grad = (
        main[...].astype(F32)
        + scale[...] * gain[...] * ng[...]
        - hidden[...].astype(F32) * pull[...]
    )
    grad_ref[...] = grad
    rows = jnp.dot(chosen[...], grad.astype(BF), preferred_element_type=F32).astype(BF)
    count, feats = out_ref.shape[0], grad.shape[1]
    for c in range(rows.shape[0] // count):
        out_ref[:, c * feats : (c + 1) * feats] = rows[c * count : (c + 1) * count]


def dispatch(ng, hidden, main, gain, scale, pull, chosen, experts):
    lead, feats = ng.shape
    slots = chosen.shape[0]
    block = lambda *shape: pl.BlockSpec(shape, lambda i: (0, 0))
    return pl.pallas_call(
        dispatch_kernel,
        grid=(1,),
        in_specs=[
            block(lead, feats),
            block(lead, feats),
            block(lead, feats),
            block(1, feats),
            block(lead, 1),
            block(lead, 1),
            block(slots, lead),
        ],
        out_specs=[block(lead, feats), block(experts, slots // experts * feats)],
        out_shape=[
            jax.ShapeDtypeStruct((lead, feats), F32),
            jax.ShapeDtypeStruct((experts, slots // experts * feats), BF),
        ],
        cost_estimate=pl.CostEstimate(
            flops=2 * slots * lead * feats, bytes_accessed=5_000_000, transcendentals=0
        ),
        compiler_params=pltpu.CompilerParams(vmem_limit_bytes=VMEM_BYTES),
        name="dispatch_rows",
    )(ng, hidden, main, gain, scale, pull, chosen)


def stacked(ref, parts, feats):
    return jnp.concatenate([ref[:, c * feats : (c + 1) * feats] for c in range(parts)], axis=0)


def down_kernel(scalars, rows_ref, down_ref, mine_ref, one_ref, three_ref, two_ref, total):
    feats = down_ref.shape[1]
    rows = stacked(rows_ref, rows_ref.shape[1] // feats, feats)
    total[...] = lax.dot_general(rows, down_ref[...], NT, preferred_element_type=F32)
    part = mine_ref.shape[0]
    for d, ref in zip((0,) + STEPS, (mine_ref, one_ref, three_ref, two_ref)):
        at = pl.multiple_of((scalars[3] + d) % NX * part, 8)
        ref[...] = total[pl.ds(at, part), :].astype(ref.dtype)


def down_sums(scalars, rows, down):
    units, feats = down.shape
    slots = rows.shape[0] * rows.shape[1] // feats
    part = slots // NX
    return pl.pallas_call(
        down_kernel,
        in_specs=[SM, VM, VM],
        out_specs=[VM] * 4,
        out_shape=[jax.ShapeDtypeStruct((part, units), F32)]
        + [jax.ShapeDtypeStruct((part, units), BF)] * 3,
        scratch_shapes=[pltpu.VMEM((slots, units), F32)],
        cost_estimate=pl.CostEstimate(
            flops=2 * slots * feats * units, bytes_accessed=4_000_000, transcendentals=0
        ),
        compiler_params=pltpu.CompilerParams(vmem_limit_bytes=VMEM_BYTES),
        name="down_sums",
    )(scalars, rows, down)


def unit_kernel(scalars, s0, s1, s3, s2, pre, w_gate, w_up, out_ref, dgate, dupper, shares):
    part, units = s0.shape
    for d, ref in zip((0,) + STEPS, (s0, s1, s3, s2)):
        rows = pl.ds(pl.multiple_of((scalars[3] + NX - d) % NX * part, 16), part)
        summed = ref[...].astype(F32)
        both = pre[rows, :]
        gate = both[:, :units].astype(F32)
        upper = both[:, units:].astype(F32)
        sig = jax.nn.sigmoid(gate)
        inside = gate * sig
        shares[rows, :] = jnp.broadcast_to(
            jnp.sum(inside * upper * summed, axis=1, keepdims=True), (part, 128)
        )
        dgate[rows, :] = (summed * upper * sig * (1.0 + gate * (1.0 - sig))).astype(BF)
        dupper[rows, :] = (summed * inside).astype(BF)
    back = lax.dot_general(dgate[...], w_gate[...], NT, preferred_element_type=F32)
    back = (back + lax.dot_general(dupper[...], w_up[...], NT, preferred_element_type=F32)).astype(BF)
    count = out_ref.shape[0]
    feats = back.shape[1]
    capacity = back.shape[0] // count
    lane = lax.broadcasted_iota(jnp.int32, (count, 128), 1)
    tail = jnp.zeros((count, 128), F32)
    for c in range(capacity):
        out_ref[:, c * feats : (c + 1) * feats] = back[c * count : (c + 1) * count]
        tail = jnp.where(lane == c, shares[c * count : (c + 1) * count, :], tail)
    out_ref[:, capacity * feats :] = tail.astype(BF)


def unit_grads(scalars, sums, pre, w_gate, w_up, experts):
    part, units = sums[0].shape
    slots = part * NX
    feats = w_gate.shape[0]
    return pl.pallas_call(
        unit_kernel,
        in_specs=[SM] + [VM] * 7,
        out_specs=VM,
        out_shape=jax.ShapeDtypeStruct((experts, slots // experts * feats + 128), BF),
        scratch_shapes=[
            pltpu.VMEM((slots, units), BF),
            pltpu.VMEM((slots, units), BF),
            pltpu.VMEM((slots, 128), F32),
        ],
        cost_estimate=pl.CostEstimate(
            flops=4 * slots * feats * units, bytes_accessed=7_000_000, transcendentals=slots * units
        ),
        compiler_params=pltpu.CompilerParams(vmem_limit_bytes=VMEM_BYTES),
        name="unit_grads",
    )(scalars, *sums, pre, w_gate, w_up)


def combine_kernel(
    back_ref, taken, chosen, gate, grad, others, scatter, routes, out_ref, gates_ref
):
    feats = grad.shape[1]
    count = back_ref.shape[0]
    capacity = back_ref.shape[1] // feats
    rows = stacked(back_ref, capacity, feats).astype(F32) * gate[...]
    high = rows.astype(BF)
    low = (rows - high.astype(F32)).astype(BF)
    added = jnp.dot(taken[...], high, preferred_element_type=F32) + jnp.dot(
        taken[...], low, preferred_element_type=F32
    )
    lead = (grad[...] + added).astype(BF)
    placed = jnp.dot(scatter[...], lead, preferred_element_type=F32)
    out_ref[...] = (others[...].astype(F32) + placed).astype(BF)
    tail = back_ref[:, capacity * feats :].astype(F32)
    by_expert = jnp.zeros((count, chosen.shape[1]), F32)
    for c in range(capacity):
        by_expert += chosen[c * count : (c + 1) * count].astype(F32) * tail[:, c : c + 1]
    ids = lax.broadcasted_iota(jnp.int32, by_expert.shape, 0)
    for k in range(2):
        named = ids == routes[k : k + 1, :]
        gates_ref[k : k + 1, :] = jnp.sum(jnp.where(named, by_expert, 0.0), axis=0, keepdims=True)


def combine(back, taken, chosen, gate, grad, others, scatter, routes):
    tokens, feats = others.shape
    return pl.pallas_call(
        combine_kernel,
        in_specs=[VM] * 8,
        out_specs=[VM, VM],
        out_shape=[
            jax.ShapeDtypeStruct((tokens, feats), BF),
            jax.ShapeDtypeStruct((2, tokens), F32),
        ],
        cost_estimate=pl.CostEstimate(
            flops=2 * tokens * feats * 1024, bytes_accessed=8_000_000, transcendentals=0
        ),
        compiler_params=pltpu.CompilerParams(vmem_limit_bytes=VMEM_BYTES),
        name="combine_rows",
    )(back, taken, chosen, gate, grad, others, scatter, routes)


def dot_nt(left, right):
    return lax.dot_general(left, right, NT, preferred_element_type=F32)


def sum_parts(mine, parts):
    moved = [expert_move(p, d, 0).astype(F32) for p, d in zip(parts, STEPS)]
    mine = ((mine + moved[0]) + (moved[1] + moved[2])).astype(BF)
    mine = (mine.astype(F32) + expert_move(mine, 0, 1).astype(F32)).astype(BF)
    return [mine] + [expert_move(mine, d, 0) for d in STEPS]


def gather_pre(pre, x, h, capacity):
    rows, width = pre.shape
    swapped = expert_move(pre, 0, 1)
    pair = jnp.where(h == 0, jnp.stack([pre, swapped]), jnp.stack([swapped, pre]))
    out = jnp.zeros((NX,) + pair.shape, pre.dtype)
    for d in (0,) + STEPS:
        piece = expert_move(pair, d, 0) if d else pair
        out = lax.dynamic_update_slice(out, piece[None], ((x + NX - d) % NX, 0, 0, 0))
    out = out.reshape(-1, capacity, width)
    return out.transpose(1, 0, 2).reshape(-1, width)


def per_device(
    hidden,
    routes,
    gates,
    saved_pre,
    w_gate,
    w_up,
    w_down,
    mtp_proj,
    mtp_gain,
    mtp_cotangent,
    main_cotangent,
):
    tokens, feats = hidden.shape
    experts = lax.axis_size("dp")
    slots = saved_pre.shape[1] * NE
    capacity = slots // experts
    lead = slots
    dp, ex = lax.axis_index("dp"), lax.axis_index("expert")
    x, h = ex // NZH, ex % NZH
    scalars = jnp.stack(
        [dp // (NZ * NC), (dp // NC) % NZ, dp % NC, x, h, x, x, x]
        + [(x + NX - d) % NX * NZH + (h + o) % NZH for d, o in PIECES]
    ).astype(jnp.int32)
    gain = mtp_gain[None, :]

    proj = gather_proj(mtp_proj.T)

    by_route = routes.T
    ids = jnp.arange(experts, dtype=jnp.int32)[:, None]
    first, second = by_route[0:1] == ids, by_route[1:2] == ids
    named = first | second
    routed = jnp.any(named, axis=0, keepdims=True)
    marks = jnp.concatenate([named, routed], axis=0).astype(BF)
    earlier = (
        lax.broadcasted_iota(jnp.int32, (tokens, tokens), 0)
        < lax.broadcasted_iota(jnp.int32, (tokens, tokens), 1)
    ).astype(BF)
    ranks = jnp.dot(marks, earlier, preferred_element_type=F32)
    number = jnp.sum(routed.astype(jnp.int32))
    ahead = ranks[experts].astype(jnp.int32)
    token = jnp.arange(tokens, dtype=jnp.int32)
    place = jnp.where(routed[0], ahead, number + token - ahead)
    order = (token[:, None] == place[None, :]).astype(BF)
    order_lead = (token[:lead, None] == place[None, :]).astype(BF)
    order_rest = (token[lead:, None] == place[None, :]).astype(BF)

    cot_lead = jnp.dot(order_lead, mtp_cotangent, preferred_element_type=F32).astype(BF)
    leads = expert_pieces(cot_lead)
    cot_rest = jnp.dot(order_rest, mtp_cotangent, preferred_element_type=F32).astype(BF)
    hid = jnp.dot(order, hidden, preferred_element_type=F32).astype(BF)
    main = jnp.dot(order, main_cotangent, preferred_element_type=F32).astype(BF)
    rests = expert_pieces(cot_rest)
    pre = gather_pre(saved_pre[0], x, h, capacity)

    seat = jnp.where(named, ranks[:experts] + 1.0, 0.0).astype(BF)
    row = lax.broadcasted_iota(jnp.int32, (slots, experts), 0)
    spread = (row % experts == lax.broadcasted_iota(jnp.int32, (slots, experts), 1)).astype(BF)
    want = (jnp.arange(slots, dtype=jnp.int32) // experts + 1).astype(F32)
    taken = jnp.dot(spread, seat, preferred_element_type=F32) == want[:, None]
    chosen = taken.astype(BF)
    gate = jnp.where(first, gates[:, 0][None, :], jnp.where(second, gates[:, 1][None, :], 0.0))
    gate = jnp.broadcast_to(gate[None], (capacity, experts, tokens)).reshape(slots, tokens)
    slot_gate = jnp.sum(jnp.where(taken, gate, 0.0), axis=1, keepdims=True)
    chosen_lead = dot_nt(chosen, order_lead).astype(BF)
    taken_lead = dot_nt(order_lead, chosen).astype(BF)
    order_back = (place[:, None] == token[None, :lead]).astype(BF)

    hid_f = hid.astype(F32)
    squares = expert_sum(jnp.sum(hid_f * hid_f, axis=1).reshape(8, tokens // 8)).reshape(tokens)
    inverse = lax.rsqrt(squares / D + EPS)
    normed = (hid_f * inverse[:, None] * gain).astype(BF)

    ng_lead, inner = first_grads(scalars, proj, leads, hid, gain)
    inner = expert_sum(inner[:, 0].reshape(1, lead)).reshape(lead)
    pull = inverse[:lead] ** 3 * inner / D
    grad_lead, outgoing = dispatch(
        ng_lead, hid, main, gain, inverse[:lead, None], pull[:, None], chosen_lead, experts
    )
    arrived = lax.all_to_all(outgoing, "dp", split_axis=0, concat_axis=0, tiled=True)

    ng_rest, inner_rest, own, other = rest_grads(scalars, proj, leads, rests, hid, gain, normed)
    grad_proj = scatter_proj(own, other)

    mine, *parts = down_sums(scalars, arrived, w_down[0])
    sums = sum_parts(mine, parts)
    back = unit_grads(scalars, sums, pre, w_gate[0], w_up[0], experts)
    returned = lax.all_to_all(back, "dp", split_axis=0, concat_axis=0, tiled=True)

    inner_rest = expert_sum(inner_rest[:, 0].reshape(1, tokens - lead)).reshape(tokens - lead)
    late = inverse[lead:]
    grad_rest = (
        main[lead:].astype(F32)
        + late[:, None] * gain * ng_rest
        - hid_f[lead:] * (late**3 * inner_rest / D)[:, None]
    ).astype(BF)
    others = lax.dot_general(
        order_rest, grad_rest, (((0,), (0,)), ((), ())), preferred_element_type=F32
    ).astype(BF)
    grad_input, gate_rows = combine(
        returned, taken_lead, chosen, slot_gate, grad_lead, others, order_back, by_route
    )
    return (grad_input, gate_rows.T.astype(BF), grad_proj)


def solution(mesh):
    return jax.shard_map(
        per_device,
        mesh=mesh,
        in_specs=(
            P("dp", "expert"),
            P("dp", None),
            P("dp", None),
            P("dp", "expert", None),
            P("dp", "expert", None),
            P("dp", "expert", None),
            P("dp", None, "expert"),
            P("expert", "dp"),
            P("expert"),
            P("dp", "expert"),
            P("dp", "expert"),
        ),
        out_specs=(P("dp", "expert"), P("dp", None), P("expert", "dp")),
        check_vma=False,
    )
```

```python
import jax
import jax.numpy as jnp
from jax import lax
from jax.experimental import pallas as pl
from jax.experimental.pallas import tpu as pltpu
from jax.sharding import PartitionSpec as P

D = 7168
EPS = 1e-06
NX, NZH = 4, 2
NY, NZ, NC = 4, 4, 2
NE = NX * NZH
ND = NY * NZ * NC
BF = jnp.bfloat16
F32 = jnp.float32
STEPS = (1, 3, 2)
Y_GROUPS = [
    [(y * NZ + z) * NC + c for y in range(NY)] for z in range(NZ) for c in range(NC)
]
X_GROUPS = [[x * NZH + h for x in range(NX)] for h in range(NZH)]
PAD = 16
HBM = pl.BlockSpec(memory_space=pltpu.HBM)
TN = (((0,), (0,)), ((), ()))
VM = pl.BlockSpec(memory_space=pltpu.VMEM)
SM = pl.BlockSpec(memory_space=pltpu.SMEM)
VMEM_BYTES = 48 * 2**20


def expert_move(value, dx, dz):
    pairs = [
        (x * NZH + h, ((x + dx) % NX) * NZH + (h + dz) % NZH) for x in range(NX) for h in range(NZH)
    ]
    return lax.ppermute(value, "expert", pairs)


def dp_move(value, dy, dz, dc):
    pairs = [
        ((y * NZ + z) * NC + c, (((y + dy) % NY) * NZ + (z + dz) % NZ) * NC + (c + dc) % NC)
        for y in range(NY)
        for z in range(NZ)
        for c in range(NC)
    ]
    return lax.ppermute(value, "dp", pairs)


def expert_sum(value):
    value = value + expert_move(value, 0, 1)
    return (value + expert_move(value, 1, 0)) + (expert_move(value, 2, 0) + expert_move(value, 3, 0))


def block_of(array, index):
    return lax.dynamic_index_in_dim(array, index, 0, keepdims=False)


def line_z(shard):
    return jnp.concatenate([shard] + [dp_move(shard, 0, d, 0) for d in STEPS], axis=0)


def gather_proj(stack):
    line = (0,) + STEPS
    half = stack.shape[0] // 2
    below, above = dp_move(stack, 1, 0, 0), dp_move(stack, NY - 1, 0, 0)
    two_below, two_above = dp_move(below[:half], 1, 0, 0), dp_move(above[half:], NY - 1, 0, 0)
    near = [
        (stack, [(0, e) for e in line]),
        (below, [(1, e) for e in line]),
        (above, [(NY - 1, e) for e in line]),
        (two_below, [(2, e) for e in line[:2]]),
        (two_above, [(2, e) for e in line[2:]]),
    ]
    return [
        (dp_move(a, 0, 0, 1) if c else a, [(d, e, c) for d, e in steps])
        for c in range(NC)
        for a, steps in near
    ]


def proj_copies(scalars, refs, layout, scratch, sems, size):
    y, z, c = scalars[0], scalars[1], scalars[2]
    copies = []
    for ref, steps in zip(refs, layout):
        for i, (dy, dz, dc) in enumerate(steps):
            at = ((y + NY - dy) % NY * NZ + (z + NZ - dz) % NZ) * NC + (c + dc) % NC
            row = pl.multiple_of(at * size, 16)
            copies.append(
                pltpu.make_async_copy(
                    ref.at[pl.ds(i * size, size)], scratch.at[pl.ds(row, size)], sems.at[len(copies)]
                )
            )
    return copies


def fill_leads(scalars, refs, scratch):
    width = scratch.shape[0] // NE
    for i, ref in enumerate(refs):
        d, o = ((0,) + STEPS)[i % NX], i // NX
        at = (scalars[3] + NX - d) % NX * NZH + (scalars[4] + o) % NZH
        scratch[pl.ds(pl.multiple_of(at * width, 64), width), :] = ref[...]


def first_kernel(layout, scalars, *refs):
    n = len(layout)
    proj_refs, cot_refs = refs[:n], refs[n : n + NE]
    hidden_ref, gain_ref, ng_ref, inner_ref, proj, cot, proj_sems = refs[n + NE :]
    size = proj.shape[0] // ND
    copies = proj_copies(scalars, proj_refs, layout, proj, proj_sems, size)
    for copy in copies:
        copy.start()
    fill_leads(scalars, cot_refs, cot)
    for copy in copies:
        copy.wait()
    tile = 128
    for i in range(ng_ref.shape[0] // tile):
        rows = slice(i * tile, (i + 1) * tile)
        part = lax.dot_general(cot[:, rows], proj[...], TN, preferred_element_type=F32)
        ng_ref[rows, :] = part
        total = jnp.sum(hidden_ref[rows, :].astype(F32) * gain_ref[...] * part, axis=1, keepdims=True)
        inner_ref[rows, :] = jnp.broadcast_to(total, (tile, 128))


def first_grads(scalars, proj, cots, hidden, gain):
    width, rows = cots[0].shape
    feats = hidden.shape[1]
    layout = [steps for _, steps in proj]
    block = lambda *shape: pl.BlockSpec(shape, lambda i: (0, 0))
    return pl.pallas_call(
        lambda *refs: first_kernel(layout, *refs),
        grid=(1,),
        in_specs=[SM] + [HBM] * len(proj) + [VM] * NE + [block(rows, feats), block(1, feats)],
        out_specs=[block(rows, feats), block(rows, 128)],
        out_shape=[
            jax.ShapeDtypeStruct((rows, feats), F32),
            jax.ShapeDtypeStruct((rows, 128), F32),
        ],
        scratch_shapes=[
            pltpu.VMEM((NE * width, feats), BF),
            pltpu.VMEM((NE * width, rows), BF),
            pltpu.SemaphoreType.DMA((ND,)),
        ],
        cost_estimate=pl.CostEstimate(
            flops=2 * rows * feats * NE * width, bytes_accessed=12_000_000, transcendentals=0
        ),
        compiler_params=pltpu.CompilerParams(vmem_limit_bytes=VMEM_BYTES),
        name="first_grads",
    )(scalars, *[a for a, _ in proj], *cots, hidden, gain)


def rest_kernel(layout, scalars, *refs):
    n = len(layout)
    proj_refs = refs[:n]
    own_ref, far_ref, hidden_ref, gain_ref, ng_ref, inner_ref, proj, cot, proj_sems = refs[n:]
    width = own_ref.shape[1]

    @pl.when(pl.program_id(0) == 0)
    def _():
        copies = proj_copies(scalars, proj_refs, layout, proj, proj_sems, width // 4)
        for copy in copies:
            copy.start()
        for copy in copies:
            copy.wait()

    for x in range(NX):
        for ref, o in ((own_ref, 0), (far_ref, 1)):
            row = pl.multiple_of((x * NZH + (scalars[4] + o) % NZH) * width, 64)
            cot[pl.ds(row, width), :] = ref[x]
    part = lax.dot_general(cot[...], proj[...], TN, preferred_element_type=F32)
    ng_ref[...] = part
    total = jnp.sum(hidden_ref[...].astype(F32) * gain_ref[...] * part, axis=1, keepdims=True)
    inner_ref[...] = jnp.broadcast_to(total, inner_ref.shape)


def rest_grads(scalars, proj, own, far, hidden, gain):
    _, width, rest = far.shape
    tokens, feats = hidden.shape
    tile = 128
    skip = (tokens - rest) // tile
    layout = [steps for _, steps in proj]
    return pl.pallas_call(
        lambda *refs: rest_kernel(layout, *refs),
        grid=(rest // tile,),
        in_specs=[SM]
        + [HBM] * len(proj)
        + [
            pl.BlockSpec((NX, width, tile), lambda i: (0, 0, i)),
            pl.BlockSpec((NX, width, tile), lambda i: (0, 0, i)),
            pl.BlockSpec((tile, feats), lambda i: (i + skip, 0)),
            pl.BlockSpec((1, feats), lambda i: (0, 0)),
        ],
        out_specs=[
            pl.BlockSpec((tile, feats), lambda i: (i, 0)),
            pl.BlockSpec((tile, 128), lambda i: (i, 0)),
        ],
        out_shape=[
            jax.ShapeDtypeStruct((rest, feats), F32),
            jax.ShapeDtypeStruct((rest, 128), F32),
        ],
        scratch_shapes=[
            pltpu.VMEM((NE * width, feats), BF),
            pltpu.VMEM((NE * width, tile), BF),
            pltpu.SemaphoreType.DMA((ND,)),
        ],
        cost_estimate=pl.CostEstimate(
            flops=2 * rest * feats * NE * width, bytes_accessed=16_000_000, transcendentals=0
        ),
        compiler_params=pltpu.CompilerParams(vmem_limit_bytes=VMEM_BYTES),
        name="rest_grads",
    )(scalars, *[a for a, _ in proj], own, far, hidden, gain)


def partial_kernel(scalars, *refs):
    lead_refs = refs[:NE]
    near_ref, far_ref, normed_ref, own_ref, other_ref, cot, leads = refs[NE:]
    width = cot.shape[0]
    lead = leads.shape[1]
    size = width // 4
    step = pl.program_id(0)

    @pl.when(step == 0)
    def _():
        fill_leads(scalars, lead_refs, leads)

    row = pl.multiple_of(scalars[8 + step] * width, 64)
    cot[:, :lead] = leads[pl.ds(row, width), :]

    @pl.when(step < NX)
    def _():
        cot[:, lead:] = near_ref[0]

    @pl.when(step >= NX)
    def _():
        cot[:, lead:] = far_ref[0]

    part = jnp.dot(cot[...], normed_ref[...], preferred_element_type=F32)
    first = scalars[2] == 0
    for z in range(2):
        zero = part[(2 * z) * size : (2 * z + 1) * size]
        one = part[(2 * z + 1) * size : (2 * z + 2) * size]
        own_ref[0, z] = jnp.where(first, zero, one)
        other_ref[0, z] = jnp.where(first, one, zero).astype(BF)


def proj_partials(scalars, leads, near, far, normed):
    tokens, feats = normed.shape
    _, width, rest = near.shape
    size = width // 4
    early = lambda i, s: (jnp.minimum(i, NX - 1), 0, 0)
    later = lambda i, s: (jnp.maximum(i - NX, 0), 0, 0)
    placed = pl.BlockSpec((1, 2, size, feats), lambda i, s: (s[8 + i], 0, 0, 0))
    return pl.pallas_call(
        partial_kernel,
        grid_spec=pltpu.PrefetchScalarGridSpec(
            num_scalar_prefetch=1,
            grid=(NE,),
            in_specs=[VM] * NE
            + [
                pl.BlockSpec((1, width, rest), early),
                pl.BlockSpec((1, width, rest), later),
                pl.BlockSpec((tokens, feats), lambda i, s: (0, 0)),
            ],
            out_specs=[placed, placed],
            scratch_shapes=[
                pltpu.VMEM((width, tokens), BF),
                pltpu.VMEM((NE * width, tokens - rest), BF),
            ],
        ),
        out_shape=[
            jax.ShapeDtypeStruct((NE, 2, size, feats), F32),
            jax.ShapeDtypeStruct((NE, 2, size, feats), BF),
        ],
        cost_estimate=pl.CostEstimate(
            flops=2 * tokens * feats * NE * width, bytes_accessed=20_000_000, transcendentals=0
        ),
        compiler_params=pltpu.CompilerParams(vmem_limit_bytes=VMEM_BYTES),
        name="proj_partials",
    )(scalars, *leads, near, far, normed)


def chip_sums(own, other, sums):
    size, feats = own.shape[2:]
    other = dp_move(other, 0, 0, 1)
    chip = (after(own, sums) + other.astype(F32)).astype(BF)
    return chip.reshape(NY, NZ, size, feats)


def over_y(chip):
    flat = chip.reshape(-1, chip.shape[3])
    out = lax.psum_scatter(flat, "dp", axis_index_groups=Y_GROUPS, tiled=True)
    return out.reshape(chip.shape[1:])


def over_z(line):
    z = (lax.axis_index("dp") // NC) % NZ
    moved = [dp_move(block_of(line, (z + d) % NZ), 0, d, 0).astype(F32) for d in STEPS]
    return ((block_of(line, z).astype(F32) + moved[0]) + (moved[1] + moved[2])).T


NT = (((1,), (1,)), ((), ()))


def dispatch_kernel(ng, hidden, main, gain, scale, pull, chosen, grad_ref, out_ref):
    grad = (
        main[...].astype(F32)
        + scale[...] * gain[...] * ng[...]
        - hidden[...].astype(F32) * pull[...]
    )
    grad_ref[...] = grad
    out_ref[...] = jnp.dot(chosen[...], grad.astype(BF), preferred_element_type=F32).astype(BF)


def dispatch(ng, hidden, main, gain, scale, pull, chosen):
    lead, feats = ng.shape
    rows = chosen.shape[0]
    block = lambda *shape: pl.BlockSpec(shape, lambda i: (0, 0))
    return pl.pallas_call(
        dispatch_kernel,
        grid=(1,),
        in_specs=[
            block(lead, feats),
            block(lead, feats),
            block(lead, feats),
            block(1, feats),
            block(lead, 1),
            block(lead, 1),
            block(rows, lead),
        ],
        out_specs=[block(lead, feats), block(rows, feats)],
        out_shape=[
            jax.ShapeDtypeStruct((lead, feats), F32),
            jax.ShapeDtypeStruct((rows, feats), BF),
        ],
        cost_estimate=pl.CostEstimate(
            flops=2 * rows * lead * feats, bytes_accessed=5_000_000, transcendentals=0
        ),
        compiler_params=pltpu.CompilerParams(vmem_limit_bytes=VMEM_BYTES),
        name="dispatch_rows",
    )(ng, hidden, main, gain, scale, pull, chosen)


def iotas(rows, columns):
    return [lax.broadcasted_iota(jnp.int32, (rows, columns), d) for d in (0, 1)]


def down_kernel(capacity, scalars, rows_ref, down_ref, mine_ref, one_ref, three_ref, two_ref, total):
    slot, row = iotas(total.shape[0], rows_ref.shape[0])
    packed = (slot // capacity * PAD + slot % capacity == row).astype(F32).astype(BF)
    rows = jnp.dot(packed, rows_ref[...], preferred_element_type=F32).astype(BF)
    total[...] = lax.dot_general(rows, down_ref[...], NT, preferred_element_type=F32)
    part = mine_ref.shape[0]
    for d, ref in zip((0,) + STEPS, (mine_ref, one_ref, three_ref, two_ref)):
        at = pl.multiple_of((scalars[3] + d) % NX * part, 8)
        ref[...] = total[pl.ds(at, part), :].astype(ref.dtype)


def down_sums(scalars, rows, down, capacity):
    units, feats = down.shape
    slots = rows.shape[0] // PAD * capacity
    part = slots // NX
    return pl.pallas_call(
        lambda *refs: down_kernel(capacity, *refs),
        in_specs=[SM, VM, VM],
        out_specs=[VM] * 4,
        out_shape=[jax.ShapeDtypeStruct((part, units), F32)]
        + [jax.ShapeDtypeStruct((part, units), BF)] * 3,
        scratch_shapes=[pltpu.VMEM((slots, units), F32)],
        cost_estimate=pl.CostEstimate(
            flops=2 * slots * feats * units, bytes_accessed=4_000_000, transcendentals=0
        ),
        compiler_params=pltpu.CompilerParams(vmem_limit_bytes=VMEM_BYTES),
        name="down_sums",
    )(scalars, rows, down)


def unit_kernel(capacity, scalars, *refs):
    sums, pres = refs[:NX], refs[NX : 2 * NX]
    w_gate, w_up, out_ref, dgate, dupper, shares = refs[2 * NX :]
    part, units = sums[0].shape
    for d, ref, pre in zip((0,) + STEPS, sums, pres):
        rows = pl.ds(pl.multiple_of((scalars[3] + NX - d) % NX * part, 16), part)
        summed = ref[...].astype(F32)
        both = pre[...]
        gate = both[:, :units].astype(F32)
        upper = both[:, units:].astype(F32)
        sig = jax.nn.sigmoid(gate)
        inside = gate * sig
        shares[rows, :] = jnp.broadcast_to(
            jnp.sum(inside * upper * summed, axis=1, keepdims=True), (part, 128)
        )
        dgate[rows, :] = (summed * upper * sig * (1.0 + gate * (1.0 - sig))).astype(BF)
        dupper[rows, :] = (summed * inside).astype(BF)
    back = lax.dot_general(dgate[...], w_gate[...], NT, preferred_element_type=F32)
    back = (back + lax.dot_general(dupper[...], w_up[...], NT, preferred_element_type=F32)).astype(BF)
    count, slots = out_ref.shape[0], back.shape[0]
    row, slot = iotas(count, slots)
    spread = (slot // capacity * PAD + slot % capacity == row).astype(F32).astype(BF)
    out_ref[...] = jnp.dot(spread, back, preferred_element_type=F32).astype(BF)
    slot, lane = iotas(slots, 128)
    along = jnp.where(slot % capacity == lane, shares[...], 0.0).astype(BF)
    spare = (slot_of(row, capacity) == iotas(count, slots)[1] // capacity).astype(F32).astype(BF)
    out_ref[:, :128] = (
        out_ref[:, :128].astype(F32) + jnp.dot(spare, along, preferred_element_type=F32)
    ).astype(BF)


def slot_of(row, capacity):
    return jnp.where(row % PAD == capacity, row // PAD, -1)


def unit_grads(scalars, sums, pre, w_gate, w_up, capacity):
    part, units = sums[0].shape
    slots = part * NX
    feats = w_gate.shape[0]
    return pl.pallas_call(
        lambda *refs: unit_kernel(capacity, *refs),
        in_specs=[SM] + [VM] * (2 * NX + 2),
        out_specs=VM,
        out_shape=jax.ShapeDtypeStruct((slots // capacity * PAD, feats), BF),
        scratch_shapes=[
            pltpu.VMEM((slots, units), BF),
            pltpu.VMEM((slots, units), BF),
            pltpu.VMEM((slots, 128), F32),
        ],
        cost_estimate=pl.CostEstimate(
            flops=4 * slots * feats * units, bytes_accessed=7_000_000, transcendentals=slots * units
        ),
        compiler_params=pltpu.CompilerParams(vmem_limit_bytes=VMEM_BYTES),
        name="unit_grads",
    )(scalars, *sums, *pre, w_gate, w_up)


def combine_kernel(
    capacity, back_ref, taken, chosen, gate, grad, others, scatter, routes, out_ref, gates_ref
):
    rows = back_ref[...].astype(F32) * gate[...]
    high = rows.astype(BF)
    low = (rows - high.astype(F32)).astype(BF)
    added = jnp.dot(taken[...], high, preferred_element_type=F32) + jnp.dot(
        taken[...], low, preferred_element_type=F32
    )
    lead = (grad[...] + added).astype(BF)
    placed = jnp.dot(scatter[...], lead, preferred_element_type=F32)
    out_ref[...] = (others[...].astype(F32) + placed).astype(BF)
    count = back_ref.shape[0]
    row, source = iotas(count, count)
    spare = (row // PAD * PAD + capacity == source).astype(F32).astype(BF)
    along = jnp.dot(spare, back_ref[:, :128], preferred_element_type=F32)
    row, lane = iotas(count, 128)
    share = jnp.sum(jnp.where(row % PAD == lane, along, 0.0), axis=1, keepdims=True)
    held = chosen[...].astype(F32) * share
    row, _ = iotas(count, held.shape[1])
    for k in range(2):
        named = row // PAD == routes[k : k + 1, :]
        gates_ref[k : k + 1, :] = jnp.sum(jnp.where(named, held, 0.0), axis=0, keepdims=True)


def combine(back, taken, chosen, gate, grad, others, scatter, routes, capacity):
    tokens, feats = others.shape
    return pl.pallas_call(
        lambda *refs: combine_kernel(capacity, *refs),
        in_specs=[VM] * 8,
        out_specs=[VM, VM],
        out_shape=[
            jax.ShapeDtypeStruct((tokens, feats), BF),
            jax.ShapeDtypeStruct((2, tokens), F32),
        ],
        cost_estimate=pl.CostEstimate(
            flops=2 * tokens * feats * 1024, bytes_accessed=8_000_000, transcendentals=0
        ),
        compiler_params=pltpu.CompilerParams(vmem_limit_bytes=VMEM_BYTES),
        name="combine_rows",
    )(back, taken, chosen, gate, grad, others, scatter, routes)


def dot_nt(left, right):
    return lax.dot_general(left, right, NT, preferred_element_type=F32)


def sum_x(mine, parts):
    moved = [expert_move(p, d, 0).astype(F32) for p, d in zip(parts, STEPS)]
    return ((mine + moved[0]) + (moved[1] + moved[2])).astype(BF)


def sum_z(mine):
    return (mine.astype(F32) + expert_move(mine, 0, 1).astype(F32)).astype(BF)


def all_x(mine):
    return [mine] + [expert_move(mine, d, 0) for d in STEPS]


def gather_x(block):
    return lax.all_gather(block, "expert", axis=0, axis_index_groups=X_GROUPS)


def after(value, *others):
    return lax.optimization_barrier((value,) + others)[0]


def per_device(
    hidden,
    routes,
    gates,
    saved_pre,
    w_gate,
    w_up,
    w_down,
    mtp_proj,
    mtp_gain,
    mtp_cotangent,
    main_cotangent,
):
    tokens, feats = hidden.shape
    experts = lax.axis_size("dp")
    slots = saved_pre.shape[1] * NE
    capacity = slots // experts
    lead = (slots + 127) // 128 * 128
    dp, ex = lax.axis_index("dp"), lax.axis_index("expert")
    x, h = ex // NZH, ex % NZH
    scalars = jnp.stack(
        [dp // (NZ * NC), (dp // NC) % NZ, dp % NC, x, h, x, x, x]
        + [i * NZH + (h + o) % NZH for o in range(NZH) for i in range(NX)]
    ).astype(jnp.int32)
    gain = mtp_gain[None, :]

    stack = line_z(mtp_proj.T)
    proj = gather_proj(stack)

    by_route = routes.T
    ids = jnp.arange(experts, dtype=jnp.int32)[:, None]
    first, second = by_route[0:1] == ids, by_route[1:2] == ids
    named = first | second
    routed = jnp.any(named, axis=0, keepdims=True)
    marks = jnp.concatenate([named, routed], axis=0).astype(BF)
    earlier = (
        lax.broadcasted_iota(jnp.int32, (tokens, tokens), 0)
        < lax.broadcasted_iota(jnp.int32, (tokens, tokens), 1)
    ).astype(BF)
    ranks = jnp.dot(marks, earlier, preferred_element_type=F32)
    number = jnp.sum(routed.astype(jnp.int32))
    ahead = ranks[experts].astype(jnp.int32)
    token = jnp.arange(tokens, dtype=jnp.int32)
    place = jnp.where(routed[0], ahead, number + token - ahead)
    order = (token[:, None] == place[None, :]).astype(BF)
    order_lead = (token[:lead, None] == place[None, :]).astype(BF)
    order_rest = (token[lead:, None] == place[None, :]).astype(BF)

    turned = mtp_cotangent.T
    cot_lead = after(dot_nt(turned, order_lead).astype(BF), stack)
    cot_rest = dot_nt(turned, order_rest).astype(BF)
    hid = jnp.dot(order, hidden, preferred_element_type=F32).astype(BF)
    main = jnp.dot(order, main_cotangent, preferred_element_type=F32).astype(BF)
    lead_swap = expert_move(cot_lead, 0, 1)
    leads = all_x(cot_lead)
    leads += all_x(after(lead_swap, hid, main, proj[1][0], proj[2][0]))
    cut = lead
    one = expert_move(after(cot_rest[:, :cut], lead_swap), 0, 1)
    two = expert_move(after(cot_rest[:, cut:], one), 0, 1)
    rest_swap = jnp.concatenate([one, two], axis=1)
    pre_own = saved_pre[0]
    pre_swap = expert_move(after(pre_own, lead_swap), 0, 1)
    pre_pair = jnp.concatenate(
        [jnp.where(h == 0, pre_own, pre_swap), jnp.where(h == 0, pre_swap, pre_own)], axis=0
    )
    near = gather_x(after(cot_rest, one, pre_pair, *leads, *[a for a, _ in proj]))

    rows = experts * PAD
    seat = jnp.where(named, ranks[:experts] + 1.0, 0.0).astype(BF)
    row = lax.broadcasted_iota(jnp.int32, (rows, experts), 0)
    spread = (row // PAD == lax.broadcasted_iota(jnp.int32, (rows, experts), 1)).astype(BF)
    want = (jnp.arange(rows, dtype=jnp.int32) % PAD + 1).astype(F32)
    taken = jnp.dot(spread, seat, preferred_element_type=F32) == want[:, None]
    chosen = taken.astype(BF)
    gate = jnp.where(first, gates[:, 0][None, :], jnp.where(second, gates[:, 1][None, :], 0.0))
    gate = jnp.broadcast_to(gate[:, None], (experts, PAD, tokens)).reshape(rows, tokens)
    slot_gate = jnp.sum(jnp.where(taken, gate, 0.0), axis=1, keepdims=True)
    chosen_lead = dot_nt(chosen, order_lead).astype(BF)
    taken_lead = dot_nt(order_lead, chosen).astype(BF)
    order_back = (place[:, None] == token[None, :lead]).astype(BF)

    hid_f = hid.astype(F32)
    squares = jnp.sum(hid_f * hid_f, axis=1)
    ng_lead, inner = first_grads(after(scalars, two), proj, leads, hid, gain)
    both = jnp.concatenate([inner[:, 0], squares]).reshape(8, -1)
    both = expert_sum(both).reshape(-1)
    inner, squares = both[:lead], both[lead:]
    inverse = lax.rsqrt(squares / D + EPS)
    pull = inverse[:lead] ** 3 * inner / D
    grad_lead, outgoing = dispatch(
        ng_lead, hid, main, gain, inverse[:lead, None], pull[:, None], chosen_lead
    )
    far = gather_x(after(rest_swap, near, outgoing))
    pre = all_x(after(pre_pair, outgoing))
    arrived = lax.all_to_all(
        outgoing.reshape(experts, PAD, feats), "dp", split_axis=0, concat_axis=0, tiled=True
    ).reshape(rows, feats)

    normed = (hid.astype(F32) * inverse[:, None] * gain).astype(BF)
    mine, *parts = down_sums(after(scalars, *pre), arrived, w_down[0], capacity)
    mine = sum_x(mine, parts)
    own, other = proj_partials(after(scalars, mine), leads, near, far, normed)
    mine = sum_z(mine)
    by_y = over_y(chip_sums(own, other, mine))
    back = unit_grads(scalars, all_x(mine), pre, w_gate[0], w_up[0], capacity)
    ng_rest, inner_rest = rest_grads(after(scalars, back), proj, near, far, hid, gain)
    inner_rest = expert_sum(inner_rest[:, 0].reshape(8, -1)).reshape(tokens - lead)
    grad_proj = over_z(by_y)
    returned = lax.all_to_all(
        back.reshape(experts, PAD, feats), "dp", split_axis=0, concat_axis=0, tiled=True
    ).reshape(rows, feats)

    late = inverse[lead:]
    grad_rest = (
        main[lead:].astype(F32)
        + late[:, None] * gain * ng_rest
        - hid[lead:].astype(F32) * (late**3 * inner_rest / D)[:, None]
    ).astype(BF)
    others = lax.dot_general(order_rest, grad_rest, TN, preferred_element_type=F32).astype(BF)
    grad_input, gate_rows = combine(
        after(returned, by_y), taken_lead, chosen, slot_gate, grad_lead, others, order_back, by_route, capacity
    )
    return (grad_input, gate_rows.T.astype(BF), grad_proj)


def solution(mesh):
    return jax.shard_map(
        per_device,
        mesh=mesh,
        in_specs=(
            P("dp", "expert"),
            P("dp", None),
            P("dp", None),
            P("dp", "expert", None),
            P("dp", "expert", None),
            P("dp", "expert", None),
            P("dp", None, "expert"),
            P("expert", "dp"),
            P("expert"),
            P("dp", "expert"),
            P("dp", "expert"),
        ),
        out_specs=(P("dp", "expert"), P("dp", None), P("expert", "dp")),
        check_vma=False,
    )
```

```python
import jax
import jax.numpy as jnp
from jax import lax
from jax.experimental import pallas as pl
from jax.experimental.pallas import tpu as pltpu
from jax.sharding import PartitionSpec as P

D = 7168
EPS = 1e-06
NX, NZH = 4, 2
NY, NZ, NC = 4, 4, 2
NE = NX * NZH
ND = NY * NZ * NC
BF = jnp.bfloat16
F32 = jnp.float32
STEPS = (1, 3, 2)
Y_GROUPS = [
    [(y * NZ + z) * NC + c for y in range(NY)] for z in range(NZ) for c in range(NC)
]
X_GROUPS = [[x * NZH + h for x in range(NX)] for h in range(NZH)]
PAD = 16
HBM = pl.BlockSpec(memory_space=pltpu.HBM)
TN = (((0,), (0,)), ((), ()))
VM = pl.BlockSpec(memory_space=pltpu.VMEM)
SM = pl.BlockSpec(memory_space=pltpu.SMEM)
VMEM_BYTES = 48 * 2**20


def expert_move(value, dx, dz):
    pairs = [
        (x * NZH + h, ((x + dx) % NX) * NZH + (h + dz) % NZH) for x in range(NX) for h in range(NZH)
    ]
    return lax.ppermute(value, "expert", pairs)


def dp_move(value, dy, dz, dc):
    pairs = [
        ((y * NZ + z) * NC + c, (((y + dy) % NY) * NZ + (z + dz) % NZ) * NC + (c + dc) % NC)
        for y in range(NY)
        for z in range(NZ)
        for c in range(NC)
    ]
    return lax.ppermute(value, "dp", pairs)


def expert_sum(value):
    value = value + expert_move(value, 0, 1)
    return (value + expert_move(value, 1, 0)) + (expert_move(value, 2, 0) + expert_move(value, 3, 0))


def block_of(array, index):
    return lax.dynamic_index_in_dim(array, index, 0, keepdims=False)


def line_z(shard):
    return jnp.concatenate([shard] + [dp_move(shard, 0, d, 0) for d in STEPS], axis=0)


def gather_proj(stack):
    line = (0,) + STEPS
    half = stack.shape[0] // 2
    below, above = dp_move(stack, 1, 0, 0), dp_move(stack, NY - 1, 0, 0)
    two_below, two_above = dp_move(below[:half], 1, 0, 0), dp_move(above[half:], NY - 1, 0, 0)
    near = [
        (stack, [(0, e) for e in line]),
        (below, [(1, e) for e in line]),
        (above, [(NY - 1, e) for e in line]),
        (two_below, [(2, e) for e in line[:2]]),
        (two_above, [(2, e) for e in line[2:]]),
    ]
    return [
        (dp_move(a, 0, 0, 1) if c else a, [(d, e, c) for d, e in steps])
        for c in range(NC)
        for a, steps in near
    ]


def proj_copies(scalars, refs, layout, scratch, sems, size):
    y, z, c = scalars[0], scalars[1], scalars[2]
    copies = []
    for ref, steps in zip(refs, layout):
        for i, (dy, dz, dc) in enumerate(steps):
            at = ((y + NY - dy) % NY * NZ + (z + NZ - dz) % NZ) * NC + (c + dc) % NC
            row = pl.multiple_of(at * size, 16)
            copies.append(
                pltpu.make_async_copy(
                    ref.at[pl.ds(i * size, size)], scratch.at[pl.ds(row, size)], sems.at[len(copies)]
                )
            )
    return copies


def lead_copies(scalars, refs, scratch, sems):
    width, lead = scratch.shape[0] // NE, scratch.shape[1]
    copies = []
    for o, ref in enumerate(refs):
        for x in range(NX):
            row = pl.multiple_of((x * NZH + (scalars[4] + o) % NZH) * width, 64)
            copies.append(
                pltpu.make_async_copy(
                    ref.at[x, :, pl.ds(0, lead)], scratch.at[pl.ds(row, width)], sems.at[len(copies)]
                )
            )
    return copies


def first_kernel(layout, scalars, *refs):
    n = len(layout)
    proj_refs, cot_refs = refs[:n], refs[n : n + NZH]
    hidden_ref, gain_ref, ng_ref, inner_ref, proj, cot, proj_sems, cot_sems = refs[n + NZH :]
    size = proj.shape[0] // ND
    copies = proj_copies(scalars, proj_refs, layout, proj, proj_sems, size)
    copies += lead_copies(scalars, cot_refs, cot, cot_sems)
    for copy in copies:
        copy.start()
    for copy in copies:
        copy.wait()
    tile = 128
    for i in range(ng_ref.shape[0] // tile):
        rows = slice(i * tile, (i + 1) * tile)
        part = lax.dot_general(cot[:, rows], proj[...], TN, preferred_element_type=F32)
        ng_ref[rows, :] = part
        total = jnp.sum(hidden_ref[rows, :].astype(F32) * gain_ref[...] * part, axis=1, keepdims=True)
        inner_ref[rows, :] = jnp.broadcast_to(total, (tile, 128))


def first_grads(scalars, proj, cots, hidden, gain):
    _, width, rows = cots[1].shape
    feats = hidden.shape[1]
    layout = [steps for _, steps in proj]
    block = lambda *shape: pl.BlockSpec(shape, lambda i: (0, 0))
    return pl.pallas_call(
        lambda *refs: first_kernel(layout, *refs),
        grid=(1,),
        in_specs=[SM] + [HBM] * (len(proj) + NZH) + [block(rows, feats), block(1, feats)],
        out_specs=[block(rows, feats), block(rows, 128)],
        out_shape=[
            jax.ShapeDtypeStruct((rows, feats), F32),
            jax.ShapeDtypeStruct((rows, 128), F32),
        ],
        scratch_shapes=[
            pltpu.VMEM((NE * width, feats), BF),
            pltpu.VMEM((NE * width, rows), BF),
            pltpu.SemaphoreType.DMA((ND,)),
            pltpu.SemaphoreType.DMA((NE,)),
        ],
        cost_estimate=pl.CostEstimate(
            flops=2 * rows * feats * NE * width, bytes_accessed=12_000_000, transcendentals=0
        ),
        compiler_params=pltpu.CompilerParams(vmem_limit_bytes=VMEM_BYTES),
        name="first_grads",
    )(scalars, *[a for a, _ in proj], *cots, hidden, gain)


def rest_kernel(layout, scalars, *refs):
    n = len(layout)
    proj_refs = refs[:n]
    own_ref, far_ref, hidden_ref, gain_ref, ng_ref, inner_ref, proj, cot, proj_sems = refs[n:]
    width = own_ref.shape[1]

    @pl.when(pl.program_id(0) == 0)
    def _():
        copies = proj_copies(scalars, proj_refs, layout, proj, proj_sems, width // 4)
        for copy in copies:
            copy.start()
        for copy in copies:
            copy.wait()

    for x in range(NX):
        for ref, o in ((own_ref, 0), (far_ref, 1)):
            row = pl.multiple_of((x * NZH + (scalars[4] + o) % NZH) * width, 64)
            cot[pl.ds(row, width), :] = ref[x]
    part = lax.dot_general(cot[...], proj[...], TN, preferred_element_type=F32)
    ng_ref[...] = part
    total = jnp.sum(hidden_ref[...].astype(F32) * gain_ref[...] * part, axis=1, keepdims=True)
    inner_ref[...] = jnp.broadcast_to(total, inner_ref.shape)


def rest_grads(scalars, proj, own, far, hidden, gain):
    _, width, rest = far.shape
    tokens, feats = hidden.shape
    tile = 128
    skip = (tokens - rest) // tile
    layout = [steps for _, steps in proj]
    return pl.pallas_call(
        lambda *refs: rest_kernel(layout, *refs),
        grid=(rest // tile,),
        in_specs=[SM]
        + [HBM] * len(proj)
        + [
            pl.BlockSpec((NX, width, tile), lambda i: (0, 0, i)),
            pl.BlockSpec((NX, width, tile), lambda i: (0, 0, i)),
            pl.BlockSpec((tile, feats), lambda i: (i + skip, 0)),
            pl.BlockSpec((1, feats), lambda i: (0, 0)),
        ],
        out_specs=[
            pl.BlockSpec((tile, feats), lambda i: (i, 0)),
            pl.BlockSpec((tile, 128), lambda i: (i, 0)),
        ],
        out_shape=[
            jax.ShapeDtypeStruct((rest, feats), F32),
            jax.ShapeDtypeStruct((rest, 128), F32),
        ],
        scratch_shapes=[
            pltpu.VMEM((NE * width, feats), BF),
            pltpu.VMEM((NE * width, tile), BF),
            pltpu.SemaphoreType.DMA((ND,)),
        ],
        cost_estimate=pl.CostEstimate(
            flops=2 * rest * feats * NE * width, bytes_accessed=16_000_000, transcendentals=0
        ),
        compiler_params=pltpu.CompilerParams(vmem_limit_bytes=VMEM_BYTES),
        name="rest_grads",
    )(scalars, *[a for a, _ in proj], own, far, hidden, gain)


def partial_kernel(scalars, *refs):
    lead_ref, near_ref, far_lead_ref, far_ref, normed_ref, own_ref, other_ref, cot = refs
    width = cot.shape[0]
    lead = lead_ref.shape[2]
    size = width // 4
    step = pl.program_id(0)

    @pl.when(step < NX)
    def _():
        cot[:, :lead] = lead_ref[0]
        cot[:, lead:] = near_ref[0]

    @pl.when(step >= NX)
    def _():
        cot[:, :lead] = far_lead_ref[0]
        cot[:, lead:] = far_ref[0]

    part = jnp.dot(cot[...], normed_ref[...], preferred_element_type=F32)
    first = scalars[2] == 0
    for z in range(2):
        zero = part[(2 * z) * size : (2 * z + 1) * size]
        one = part[(2 * z + 1) * size : (2 * z + 2) * size]
        own_ref[0, z] = jnp.where(first, zero, one)
        other_ref[0, z] = jnp.where(first, one, zero).astype(BF)


def proj_partials(scalars, lead, near, far_lead, far, normed):
    tokens, feats = normed.shape
    _, width, rest = near.shape
    size = width // 4
    early = lambda i, s: (jnp.minimum(i, NX - 1), 0, 0)
    later = lambda i, s: (jnp.maximum(i - NX, 0), 0, 0)
    placed = pl.BlockSpec((1, 2, size, feats), lambda i, s: (s[8 + i], 0, 0, 0))
    return pl.pallas_call(
        partial_kernel,
        grid_spec=pltpu.PrefetchScalarGridSpec(
            num_scalar_prefetch=1,
            grid=(NE,),
            in_specs=[
                pl.BlockSpec((1, width, tokens - rest), early),
                pl.BlockSpec((1, width, rest), early),
                pl.BlockSpec((1, width, tokens - rest), later),
                pl.BlockSpec((1, width, rest), later),
                pl.BlockSpec((tokens, feats), lambda i, s: (0, 0)),
            ],
            out_specs=[placed, placed],
            scratch_shapes=[pltpu.VMEM((width, tokens), BF)],
        ),
        out_shape=[
            jax.ShapeDtypeStruct((NE, 2, size, feats), F32),
            jax.ShapeDtypeStruct((NE, 2, size, feats), BF),
        ],
        cost_estimate=pl.CostEstimate(
            flops=2 * tokens * feats * NE * width, bytes_accessed=20_000_000, transcendentals=0
        ),
        compiler_params=pltpu.CompilerParams(vmem_limit_bytes=VMEM_BYTES),
        name="proj_partials",
    )(scalars, lead, near, far_lead, far, normed)


def chip_sums(own, other, sums):
    size, feats = own.shape[2:]
    other = dp_move(other, 0, 0, 1)
    chip = (after(own, sums) + other.astype(F32)).astype(BF)
    return chip.reshape(NY, NZ, size, feats)


def over_y(chip):
    flat = chip.reshape(-1, chip.shape[3])
    out = lax.psum_scatter(flat, "dp", axis_index_groups=Y_GROUPS, tiled=True)
    return out.reshape(chip.shape[1:])


def over_z(line):
    z = (lax.axis_index("dp") // NC) % NZ
    moved = [dp_move(block_of(line, (z + d) % NZ), 0, d, 0).astype(F32) for d in STEPS]
    return ((block_of(line, z).astype(F32) + moved[0]) + (moved[1] + moved[2])).T


NT = (((1,), (1,)), ((), ()))


def dispatch_kernel(ng, hidden, main, gain, scale, pull, chosen, grad_ref, out_ref):
    grad = (
        main[...].astype(F32)
        + scale[...] * gain[...] * ng[...]
        - hidden[...].astype(F32) * pull[...]
    )
    grad_ref[...] = grad
    out_ref[...] = jnp.dot(chosen[...], grad.astype(BF), preferred_element_type=F32).astype(BF)


def dispatch(ng, hidden, main, gain, scale, pull, chosen):
    lead, feats = ng.shape
    rows = chosen.shape[0]
    block = lambda *shape: pl.BlockSpec(shape, lambda i: (0, 0))
    return pl.pallas_call(
        dispatch_kernel,
        grid=(1,),
        in_specs=[
            block(lead, feats),
            block(lead, feats),
            block(lead, feats),
            block(1, feats),
            block(lead, 1),
            block(lead, 1),
            block(rows, lead),
        ],
        out_specs=[block(lead, feats), block(rows, feats)],
        out_shape=[
            jax.ShapeDtypeStruct((lead, feats), F32),
            jax.ShapeDtypeStruct((rows, feats), BF),
        ],
        cost_estimate=pl.CostEstimate(
            flops=2 * rows * lead * feats, bytes_accessed=5_000_000, transcendentals=0
        ),
        compiler_params=pltpu.CompilerParams(vmem_limit_bytes=VMEM_BYTES),
        name="dispatch_rows",
    )(ng, hidden, main, gain, scale, pull, chosen)


def iotas(rows, columns):
    return [lax.broadcasted_iota(jnp.int32, (rows, columns), d) for d in (0, 1)]


def down_kernel(capacity, scalars, rows_ref, down_ref, mine_ref, one_ref, three_ref, two_ref, total):
    slot, row = iotas(total.shape[0], rows_ref.shape[0])
    packed = (slot // capacity * PAD + slot % capacity == row).astype(F32).astype(BF)
    rows = jnp.dot(packed, rows_ref[...], preferred_element_type=F32).astype(BF)
    total[...] = lax.dot_general(rows, down_ref[...], NT, preferred_element_type=F32)
    part = mine_ref.shape[0]
    for d, ref in zip((0,) + STEPS, (mine_ref, one_ref, three_ref, two_ref)):
        at = pl.multiple_of((scalars[3] + d) % NX * part, 8)
        ref[...] = total[pl.ds(at, part), :].astype(ref.dtype)


def down_sums(scalars, rows, down, capacity):
    units, feats = down.shape
    slots = rows.shape[0] // PAD * capacity
    part = slots // NX
    return pl.pallas_call(
        lambda *refs: down_kernel(capacity, *refs),
        in_specs=[SM, VM, VM],
        out_specs=[VM] * 4,
        out_shape=[jax.ShapeDtypeStruct((part, units), F32)]
        + [jax.ShapeDtypeStruct((part, units), BF)] * 3,
        scratch_shapes=[pltpu.VMEM((slots, units), F32)],
        cost_estimate=pl.CostEstimate(
            flops=2 * slots * feats * units, bytes_accessed=4_000_000, transcendentals=0
        ),
        compiler_params=pltpu.CompilerParams(vmem_limit_bytes=VMEM_BYTES),
        name="down_sums",
    )(scalars, rows, down)


def unit_kernel(capacity, scalars, *refs):
    sums, pres = refs[:NX], refs[NX : 2 * NX]
    w_gate, w_up, out_ref, dgate, dupper, shares = refs[2 * NX :]
    part, units = sums[0].shape
    for d, ref, pre in zip((0,) + STEPS, sums, pres):
        rows = pl.ds(pl.multiple_of((scalars[3] + NX - d) % NX * part, 16), part)
        summed = ref[...].astype(F32)
        both = pre[...]
        gate = both[:, :units].astype(F32)
        upper = both[:, units:].astype(F32)
        sig = jax.nn.sigmoid(gate)
        inside = gate * sig
        shares[rows, :] = jnp.broadcast_to(
            jnp.sum(inside * upper * summed, axis=1, keepdims=True), (part, 128)
        )
        dgate[rows, :] = (summed * upper * sig * (1.0 + gate * (1.0 - sig))).astype(BF)
        dupper[rows, :] = (summed * inside).astype(BF)
    back = lax.dot_general(dgate[...], w_gate[...], NT, preferred_element_type=F32)
    back = (back + lax.dot_general(dupper[...], w_up[...], NT, preferred_element_type=F32)).astype(BF)
    count, slots = out_ref.shape[0], back.shape[0]
    row, slot = iotas(count, slots)
    spread = (slot // capacity * PAD + slot % capacity == row).astype(F32).astype(BF)
    out_ref[...] = jnp.dot(spread, back, preferred_element_type=F32).astype(BF)
    slot, lane = iotas(slots, 128)
    along = jnp.where(slot % capacity == lane, shares[...], 0.0).astype(BF)
    spare = (slot_of(row, capacity) == iotas(count, slots)[1] // capacity).astype(F32).astype(BF)
    out_ref[:, :128] = (
        out_ref[:, :128].astype(F32) + jnp.dot(spare, along, preferred_element_type=F32)
    ).astype(BF)


def slot_of(row, capacity):
    return jnp.where(row % PAD == capacity, row // PAD, -1)


def unit_grads(scalars, sums, pre, w_gate, w_up, capacity):
    part, units = sums[0].shape
    slots = part * NX
    feats = w_gate.shape[0]
    return pl.pallas_call(
        lambda *refs: unit_kernel(capacity, *refs),
        in_specs=[SM] + [VM] * (2 * NX + 2),
        out_specs=VM,
        out_shape=jax.ShapeDtypeStruct((slots // capacity * PAD, feats), BF),
        scratch_shapes=[
            pltpu.VMEM((slots, units), BF),
            pltpu.VMEM((slots, units), BF),
            pltpu.VMEM((slots, 128), F32),
        ],
        cost_estimate=pl.CostEstimate(
            flops=4 * slots * feats * units, bytes_accessed=7_000_000, transcendentals=slots * units
        ),
        compiler_params=pltpu.CompilerParams(vmem_limit_bytes=VMEM_BYTES),
        name="unit_grads",
    )(scalars, *sums, *pre, w_gate, w_up)


def combine_kernel(
    capacity, back_ref, taken, chosen, gate, grad, others, scatter, routes, out_ref, gates_ref
):
    rows = back_ref[...].astype(F32) * gate[...]
    high = rows.astype(BF)
    low = (rows - high.astype(F32)).astype(BF)
    added = jnp.dot(taken[...], high, preferred_element_type=F32) + jnp.dot(
        taken[...], low, preferred_element_type=F32
    )
    lead = (grad[...] + added).astype(BF)
    placed = jnp.dot(scatter[...], lead, preferred_element_type=F32)
    out_ref[...] = (others[...].astype(F32) + placed).astype(BF)
    count = back_ref.shape[0]
    row, source = iotas(count, count)
    spare = (row // PAD * PAD + capacity == source).astype(F32).astype(BF)
    along = jnp.dot(spare, back_ref[:, :128], preferred_element_type=F32)
    row, lane = iotas(count, 128)
    share = jnp.sum(jnp.where(row % PAD == lane, along, 0.0), axis=1, keepdims=True)
    held = chosen[...].astype(F32) * share
    row, _ = iotas(count, held.shape[1])
    for k in range(2):
        named = row // PAD == routes[k : k + 1, :]
        gates_ref[k : k + 1, :] = jnp.sum(jnp.where(named, held, 0.0), axis=0, keepdims=True)


def combine(back, taken, chosen, gate, grad, others, scatter, routes, capacity):
    tokens, feats = others.shape
    return pl.pallas_call(
        lambda *refs: combine_kernel(capacity, *refs),
        in_specs=[VM] * 8,
        out_specs=[VM, VM],
        out_shape=[
            jax.ShapeDtypeStruct((tokens, feats), BF),
            jax.ShapeDtypeStruct((2, tokens), F32),
        ],
        cost_estimate=pl.CostEstimate(
            flops=2 * tokens * feats * 1024, bytes_accessed=8_000_000, transcendentals=0
        ),
        compiler_params=pltpu.CompilerParams(vmem_limit_bytes=VMEM_BYTES),
        name="combine_rows",
    )(back, taken, chosen, gate, grad, others, scatter, routes)


def dot_nt(left, right):
    return lax.dot_general(left, right, NT, preferred_element_type=F32)


def sum_x(mine, parts):
    moved = [expert_move(p, d, 0).astype(F32) for p, d in zip(parts, STEPS)]
    return ((mine + moved[0]) + (moved[1] + moved[2])).astype(BF)


def sum_z(mine):
    return (mine.astype(F32) + expert_move(mine, 0, 1).astype(F32)).astype(BF)


def all_x(mine):
    return [mine] + [expert_move(mine, d, 0) for d in STEPS]


def gather_x(block):
    return lax.all_gather(block, "expert", axis=0, axis_index_groups=X_GROUPS)


def after(value, *others):
    return lax.optimization_barrier((value,) + others)[0]


def per_device(
    hidden,
    routes,
    gates,
    saved_pre,
    w_gate,
    w_up,
    w_down,
    mtp_proj,
    mtp_gain,
    mtp_cotangent,
    main_cotangent,
):
    tokens, feats = hidden.shape
    experts = lax.axis_size("dp")
    slots = saved_pre.shape[1] * NE
    capacity = slots // experts
    lead = (slots + 127) // 128 * 128
    dp, ex = lax.axis_index("dp"), lax.axis_index("expert")
    x, h = ex // NZH, ex % NZH
    scalars = jnp.stack(
        [dp // (NZ * NC), (dp // NC) % NZ, dp % NC, x, h, x, x, x]
        + [i * NZH + (h + o) % NZH for o in range(NZH) for i in range(NX)]
    ).astype(jnp.int32)
    gain = mtp_gain[None, :]

    stack = line_z(mtp_proj.T)
    proj = gather_proj(stack)

    by_route = routes.T
    ids = jnp.arange(experts, dtype=jnp.int32)[:, None]
    first, second = by_route[0:1] == ids, by_route[1:2] == ids
    named = first | second
    routed = jnp.any(named, axis=0, keepdims=True)
    marks = jnp.concatenate([named, routed], axis=0).astype(BF)
    earlier = (
        lax.broadcasted_iota(jnp.int32, (tokens, tokens), 0)
        < lax.broadcasted_iota(jnp.int32, (tokens, tokens), 1)
    ).astype(BF)
    ranks = jnp.dot(marks, earlier, preferred_element_type=F32)
    number = jnp.sum(routed.astype(jnp.int32))
    ahead = ranks[experts].astype(jnp.int32)
    token = jnp.arange(tokens, dtype=jnp.int32)
    place = jnp.where(routed[0], ahead, number + token - ahead)
    order = (token[:, None] == place[None, :]).astype(BF)
    order_lead = (token[:lead, None] == place[None, :]).astype(BF)
    order_rest = (token[lead:, None] == place[None, :]).astype(BF)

    turned = mtp_cotangent.T
    cot_lead = after(dot_nt(turned, order_lead).astype(BF), stack)
    cot_rest = dot_nt(turned, order_rest).astype(BF)
    own_lead = gather_x(cot_lead)
    lead_swap = expert_move(cot_lead, 0, 1)
    hid = jnp.dot(order, hidden, preferred_element_type=F32).astype(BF)
    main = jnp.dot(order, main_cotangent, preferred_element_type=F32).astype(BF)
    far_lead = gather_x(after(lead_swap, own_lead, hid, main, proj[1][0], proj[2][0]))
    one = expert_move(after(cot_rest[:, :lead], lead_swap), 0, 1)
    two = expert_move(after(cot_rest[:, lead:], one), 0, 1)
    rest_swap = jnp.concatenate([one, two], axis=1)
    pre_own = saved_pre[0]
    pre_swap = expert_move(after(pre_own, lead_swap), 0, 1)
    pre_pair = jnp.concatenate(
        [jnp.where(h == 0, pre_own, pre_swap), jnp.where(h == 0, pre_swap, pre_own)], axis=0
    )
    near = gather_x(after(cot_rest, far_lead, one, pre_pair, *[a for a, _ in proj]))
    rows = experts * PAD
    seat = jnp.where(named, ranks[:experts] + 1.0, 0.0).astype(BF)
    row = lax.broadcasted_iota(jnp.int32, (rows, experts), 0)
    spread = (row // PAD == lax.broadcasted_iota(jnp.int32, (rows, experts), 1)).astype(BF)
    want = (jnp.arange(rows, dtype=jnp.int32) % PAD + 1).astype(F32)
    taken = jnp.dot(spread, seat, preferred_element_type=F32) == want[:, None]
    chosen = taken.astype(BF)
    gate = jnp.where(first, gates[:, 0][None, :], jnp.where(second, gates[:, 1][None, :], 0.0))
    gate = jnp.broadcast_to(gate[:, None], (experts, PAD, tokens)).reshape(rows, tokens)
    slot_gate = jnp.sum(jnp.where(taken, gate, 0.0), axis=1, keepdims=True)
    chosen_lead = dot_nt(chosen, order_lead).astype(BF)
    taken_lead = dot_nt(order_lead, chosen).astype(BF)
    order_back = (place[:, None] == token[None, :lead]).astype(BF)

    hid_f = hid.astype(F32)
    squares = jnp.sum(hid_f * hid_f, axis=1)
    ng_lead, inner = first_grads(scalars, proj, (own_lead, far_lead), hid, gain)
    both = jnp.concatenate([inner[:, 0], squares]).reshape(8, -1)
    both = expert_sum(both).reshape(-1)
    inner, squares = both[:lead], both[lead:]
    inverse = lax.rsqrt(squares / D + EPS)
    pull = inverse[:lead] ** 3 * inner / D
    grad_lead, outgoing = dispatch(
        ng_lead, hid, main, gain, inverse[:lead, None], pull[:, None], chosen_lead
    )
    far = gather_x(after(rest_swap, near, outgoing))
    pre = all_x(after(pre_pair, outgoing))
    arrived = lax.all_to_all(
        outgoing.reshape(experts, PAD, feats), "dp", split_axis=0, concat_axis=0, tiled=True
    ).reshape(rows, feats)

    normed = (hid.astype(F32) * inverse[:, None] * gain).astype(BF)
    mine, *parts = down_sums(after(scalars, *pre), arrived, w_down[0], capacity)
    mine = sum_x(mine, parts)
    own, other = proj_partials(after(scalars, mine), own_lead, near, far_lead, far, normed)
    mine = sum_z(mine)
    by_y = over_y(chip_sums(own, other, mine))
    back = unit_grads(scalars, all_x(mine), pre, w_gate[0], w_up[0], capacity)
    ng_rest, inner_rest = rest_grads(after(scalars, back), proj, near, far, hid, gain)
    inner_rest = expert_sum(inner_rest[:, 0].reshape(8, -1)).reshape(tokens - lead)
    grad_proj = over_z(by_y)
    returned = lax.all_to_all(
        back.reshape(experts, PAD, feats), "dp", split_axis=0, concat_axis=0, tiled=True
    ).reshape(rows, feats)

    late = inverse[lead:]
    grad_rest = (
        main[lead:].astype(F32)
        + late[:, None] * gain * ng_rest
        - hid[lead:].astype(F32) * (late**3 * inner_rest / D)[:, None]
    ).astype(BF)
    others = lax.dot_general(order_rest, grad_rest, TN, preferred_element_type=F32).astype(BF)
    grad_input, gate_rows = combine(
        after(returned, by_y), taken_lead, chosen, slot_gate, grad_lead, others, order_back, by_route, capacity
    )
    return (grad_input, gate_rows.T.astype(BF), grad_proj)


def solution(mesh):
    return jax.shard_map(
        per_device,
        mesh=mesh,
        in_specs=(
            P("dp", "expert"),
            P("dp", None),
            P("dp", None),
            P("dp", "expert", None),
            P("dp", "expert", None),
            P("dp", "expert", None),
            P("dp", None, "expert"),
            P("expert", "dp"),
            P("expert"),
            P("dp", "expert"),
            P("dp", "expert"),
        ),
        out_specs=(P("dp", "expert"), P("dp", None), P("expert", "dp")),
        check_vma=False,
    )
```

```python
import jax
import jax.numpy as jnp
from jax import lax
from jax.experimental import pallas as pl
from jax.experimental.pallas import tpu as pltpu
from jax.sharding import PartitionSpec as P

D = 7168
EPS = 1e-06
NX, NZH = 4, 2
NY, NZ, NC = 4, 4, 2
NE = NX * NZH
ND = NY * NZ * NC
BF = jnp.bfloat16
F32 = jnp.float32
STEPS = (1, 3, 2)
Y_GROUPS = [
    [(y * NZ + z) * NC + c for y in range(NY)] for z in range(NZ) for c in range(NC)
]
X_GROUPS = [[x * NZH + h for x in range(NX)] for h in range(NZH)]
PAD = 16
HBM = pl.BlockSpec(memory_space=pltpu.HBM)
TN = (((0,), (0,)), ((), ()))
VM = pl.BlockSpec(memory_space=pltpu.VMEM)
SM = pl.BlockSpec(memory_space=pltpu.SMEM)
VMEM_BYTES = 48 * 2**20


def expert_move(value, dx, dz):
    pairs = [
        (x * NZH + h, ((x + dx) % NX) * NZH + (h + dz) % NZH) for x in range(NX) for h in range(NZH)
    ]
    return lax.ppermute(value, "expert", pairs)


def dp_move(value, dy, dz, dc):
    pairs = [
        ((y * NZ + z) * NC + c, (((y + dy) % NY) * NZ + (z + dz) % NZ) * NC + (c + dc) % NC)
        for y in range(NY)
        for z in range(NZ)
        for c in range(NC)
    ]
    return lax.ppermute(value, "dp", pairs)


def expert_sum(value):
    value = value + expert_move(value, 0, 1)
    return (value + expert_move(value, 1, 0)) + (expert_move(value, 2, 0) + expert_move(value, 3, 0))


def block_of(array, index):
    return lax.dynamic_index_in_dim(array, index, 0, keepdims=False)


def line_z(shard):
    return jnp.concatenate([shard] + [dp_move(shard, 0, d, 0) for d in STEPS], axis=0)


def gather_proj(stack):
    line = (0,) + STEPS
    half = stack.shape[0] // 2
    below, above = dp_move(stack, 1, 0, 0), dp_move(stack, NY - 1, 0, 0)
    two_below, two_above = dp_move(below[:half], 1, 0, 0), dp_move(above[half:], NY - 1, 0, 0)
    near = [
        (stack, [(0, e) for e in line]),
        (below, [(1, e) for e in line]),
        (above, [(NY - 1, e) for e in line]),
        (two_below, [(2, e) for e in line[:2]]),
        (two_above, [(2, e) for e in line[2:]]),
    ]
    return [
        (dp_move(a, 0, 0, 1) if c else a, [(d, e, c) for d, e in steps])
        for c in range(NC)
        for a, steps in near
    ]


def proj_copies(scalars, refs, layout, scratch, sems, size):
    y, z, c = scalars[0], scalars[1], scalars[2]
    copies = []
    for ref, steps in zip(refs, layout):
        for i, (dy, dz, dc) in enumerate(steps):
            at = ((y + NY - dy) % NY * NZ + (z + NZ - dz) % NZ) * NC + (c + dc) % NC
            row = pl.multiple_of(at * size, 16)
            copies.append(
                pltpu.make_async_copy(
                    ref.at[pl.ds(i * size, size)], scratch.at[pl.ds(row, size)], sems.at[len(copies)]
                )
            )
    return copies


def lead_copies(scalars, refs, scratch, sems):
    width, lead = scratch.shape[0] // NE, scratch.shape[1]
    copies = []
    for o, ref in enumerate(refs):
        for x in range(NX):
            row = pl.multiple_of((x * NZH + (scalars[4] + o) % NZH) * width, 64)
            copies.append(
                pltpu.make_async_copy(
                    ref.at[x, :, pl.ds(0, lead)], scratch.at[pl.ds(row, width)], sems.at[len(copies)]
                )
            )
    return copies


def first_kernel(layout, scalars, *refs):
    n = len(layout)
    proj_refs, cot_refs = refs[:n], refs[n : n + NZH]
    hidden_ref, gain_ref, ng_ref, inner_ref, proj, cot, proj_sems, cot_sems = refs[n + NZH :]
    size = proj.shape[0] // ND
    copies = proj_copies(scalars, proj_refs, layout, proj, proj_sems, size)
    copies += lead_copies(scalars, cot_refs, cot, cot_sems)
    for copy in copies:
        copy.start()
    for copy in copies:
        copy.wait()
    part = lax.dot_general(cot[...], proj[...], TN, preferred_element_type=F32)
    ng_ref[...] = part
    total = jnp.sum(hidden_ref[...].astype(F32) * gain_ref[...] * part, axis=1, keepdims=True)
    inner_ref[...] = jnp.broadcast_to(total, inner_ref.shape)


def first_grads(scalars, proj, cots, hidden, gain):
    _, width, rows = cots[1].shape
    feats = hidden.shape[1]
    layout = [steps for _, steps in proj]
    block = lambda *shape: pl.BlockSpec(shape, lambda i: (0, 0))
    return pl.pallas_call(
        lambda *refs: first_kernel(layout, *refs),
        grid=(1,),
        in_specs=[SM] + [HBM] * (len(proj) + NZH) + [block(rows, feats), block(1, feats)],
        out_specs=[block(rows, feats), block(rows, 128)],
        out_shape=[
            jax.ShapeDtypeStruct((rows, feats), F32),
            jax.ShapeDtypeStruct((rows, 128), F32),
        ],
        scratch_shapes=[
            pltpu.VMEM((NE * width, feats), BF),
            pltpu.VMEM((NE * width, rows), BF),
            pltpu.SemaphoreType.DMA((ND,)),
            pltpu.SemaphoreType.DMA((NE,)),
        ],
        cost_estimate=pl.CostEstimate(
            flops=2 * rows * feats * NE * width, bytes_accessed=12_000_000, transcendentals=0
        ),
        compiler_params=pltpu.CompilerParams(vmem_limit_bytes=VMEM_BYTES),
        name="first_grads",
    )(scalars, *[a for a, _ in proj], *cots, hidden, gain)


def rest_kernel(layout, scalars, *refs):
    n = len(layout)
    proj_refs = refs[:n]
    own_ref, far_ref, hidden_ref, gain_ref, ng_ref, inner_ref, proj, cot, proj_sems = refs[n:]
    width = own_ref.shape[1]

    @pl.when(pl.program_id(0) == 0)
    def _():
        copies = proj_copies(scalars, proj_refs, layout, proj, proj_sems, width // 4)
        for copy in copies:
            copy.start()
        for copy in copies:
            copy.wait()

    for x in range(NX):
        for ref, o in ((own_ref, 0), (far_ref, 1)):
            row = pl.multiple_of((x * NZH + (scalars[4] + o) % NZH) * width, 64)
            cot[pl.ds(row, width), :] = ref[x]
    part = lax.dot_general(cot[...], proj[...], TN, preferred_element_type=F32)
    ng_ref[...] = part
    late = hidden_ref[hidden_ref.shape[0] - part.shape[0] :, :].astype(F32)
    total = jnp.sum(late * gain_ref[...] * part, axis=1, keepdims=True)
    inner_ref[...] = jnp.broadcast_to(total, inner_ref.shape)


def rest_grads(scalars, proj, own, far, hidden, gain):
    _, width, rest = far.shape
    tokens, feats = hidden.shape
    tile = rest
    layout = [steps for _, steps in proj]
    return pl.pallas_call(
        lambda *refs: rest_kernel(layout, *refs),
        grid=(rest // tile,),
        in_specs=[SM]
        + [HBM] * len(proj)
        + [
            pl.BlockSpec((NX, width, tile), lambda i: (0, 0, i)),
            pl.BlockSpec((NX, width, tile), lambda i: (0, 0, i)),
            pl.BlockSpec((tokens, feats), lambda i: (0, 0)),
            pl.BlockSpec((1, feats), lambda i: (0, 0)),
        ],
        out_specs=[
            pl.BlockSpec((tile, feats), lambda i: (i, 0)),
            pl.BlockSpec((tile, 128), lambda i: (i, 0)),
        ],
        out_shape=[
            jax.ShapeDtypeStruct((rest, feats), F32),
            jax.ShapeDtypeStruct((rest, 128), F32),
        ],
        scratch_shapes=[
            pltpu.VMEM((NE * width, feats), BF),
            pltpu.VMEM((NE * width, tile), BF),
            pltpu.SemaphoreType.DMA((ND,)),
        ],
        cost_estimate=pl.CostEstimate(
            flops=2 * rest * feats * NE * width, bytes_accessed=16_000_000, transcendentals=0
        ),
        compiler_params=pltpu.CompilerParams(vmem_limit_bytes=VMEM_BYTES),
        name="rest_grads",
    )(scalars, *[a for a, _ in proj], own, far, hidden, gain)


def partial_kernel(scalars, *refs):
    lead_ref, near_ref, far_lead_ref, far_ref, normed_ref, own_ref, other_ref, cot = refs
    width = cot.shape[0]
    lead = lead_ref.shape[2]
    size = width // 4
    step = pl.program_id(0)

    @pl.when(step < NX)
    def _():
        cot[:, :lead] = lead_ref[0]
        cot[:, lead:] = near_ref[0]

    @pl.when(step >= NX)
    def _():
        cot[:, :lead] = far_lead_ref[0]
        cot[:, lead:] = far_ref[0]

    part = jnp.dot(cot[...], normed_ref[...], preferred_element_type=F32)
    first = scalars[2] == 0
    for z in range(2):
        zero = part[(2 * z) * size : (2 * z + 1) * size]
        one = part[(2 * z + 1) * size : (2 * z + 2) * size]
        own_ref[0, z] = jnp.where(first, zero, one)
        other_ref[0, z] = jnp.where(first, one, zero).astype(BF)


def proj_partials(scalars, lead, near, far_lead, far, normed):
    tokens, feats = normed.shape
    _, width, rest = near.shape
    size = width // 4
    early = lambda i, s: (jnp.minimum(i, NX - 1), 0, 0)
    later = lambda i, s: (jnp.maximum(i - NX, 0), 0, 0)
    placed = pl.BlockSpec((1, 2, size, feats), lambda i, s: (s[8 + i], 0, 0, 0))
    return pl.pallas_call(
        partial_kernel,
        grid_spec=pltpu.PrefetchScalarGridSpec(
            num_scalar_prefetch=1,
            grid=(NE,),
            in_specs=[
                pl.BlockSpec((1, width, tokens - rest), early),
                pl.BlockSpec((1, width, rest), early),
                pl.BlockSpec((1, width, tokens - rest), later),
                pl.BlockSpec((1, width, rest), later),
                pl.BlockSpec((tokens, feats), lambda i, s: (0, 0)),
            ],
            out_specs=[placed, placed],
            scratch_shapes=[pltpu.VMEM((width, tokens), BF)],
        ),
        out_shape=[
            jax.ShapeDtypeStruct((NE, 2, size, feats), F32),
            jax.ShapeDtypeStruct((NE, 2, size, feats), BF),
        ],
        cost_estimate=pl.CostEstimate(
            flops=2 * tokens * feats * NE * width, bytes_accessed=20_000_000, transcendentals=0
        ),
        compiler_params=pltpu.CompilerParams(vmem_limit_bytes=VMEM_BYTES),
        name="proj_partials",
    )(scalars, lead, near, far_lead, far, normed)


def chip_sums(own, other, sums):
    size, feats = own.shape[2:]
    other = dp_move(other, 0, 0, 1)
    chip = (after(own, sums) + other.astype(F32)).astype(BF)
    return chip.reshape(NY, NZ, size, feats)


def over_y(chip):
    flat = chip.reshape(-1, chip.shape[3])
    out = lax.psum_scatter(flat, "dp", axis_index_groups=Y_GROUPS, tiled=True)
    return out.reshape(chip.shape[1:])


def over_z(line):
    z = (lax.axis_index("dp") // NC) % NZ
    moved = [dp_move(block_of(line, (z + d) % NZ), 0, d, 0).astype(F32) for d in STEPS]
    return ((block_of(line, z).astype(F32) + moved[0]) + (moved[1] + moved[2])).T


NT = (((1,), (1,)), ((), ()))


def dispatch_kernel(ng, hidden, main, gain, scale, pull, chosen, grad_ref, out_ref):
    grad = (
        main[...].astype(F32)
        + scale[...] * gain[...] * ng[...]
        - hidden[...].astype(F32) * pull[...]
    )
    grad_ref[...] = grad
    out_ref[...] = jnp.dot(chosen[...], grad.astype(BF), preferred_element_type=F32).astype(BF)


def dispatch(ng, hidden, main, gain, scale, pull, chosen):
    lead, feats = ng.shape
    rows = chosen.shape[0]
    block = lambda *shape: pl.BlockSpec(shape, lambda i: (0, 0))
    return pl.pallas_call(
        dispatch_kernel,
        grid=(1,),
        in_specs=[
            block(lead, feats),
            block(lead, feats),
            block(lead, feats),
            block(1, feats),
            block(lead, 1),
            block(lead, 1),
            block(rows, lead),
        ],
        out_specs=[block(lead, feats), block(rows, feats)],
        out_shape=[
            jax.ShapeDtypeStruct((lead, feats), F32),
            jax.ShapeDtypeStruct((rows, feats), BF),
        ],
        cost_estimate=pl.CostEstimate(
            flops=2 * rows * lead * feats, bytes_accessed=5_000_000, transcendentals=0
        ),
        compiler_params=pltpu.CompilerParams(vmem_limit_bytes=VMEM_BYTES),
        name="dispatch_rows",
    )(ng, hidden, main, gain, scale, pull, chosen)


def iotas(rows, columns):
    return [lax.broadcasted_iota(jnp.int32, (rows, columns), d) for d in (0, 1)]


def down_kernel(capacity, scalars, rows_ref, down_ref, mine_ref, one_ref, three_ref, two_ref, total):
    slot, row = iotas(total.shape[0], rows_ref.shape[0])
    packed = (slot // capacity * PAD + slot % capacity == row).astype(F32).astype(BF)
    rows = jnp.dot(packed, rows_ref[...], preferred_element_type=F32).astype(BF)
    total[...] = lax.dot_general(rows, down_ref[...], NT, preferred_element_type=F32)
    part = mine_ref.shape[0]
    for d, ref in zip((0,) + STEPS, (mine_ref, one_ref, three_ref, two_ref)):
        at = pl.multiple_of((scalars[3] + d) % NX * part, 8)
        ref[...] = total[pl.ds(at, part), :].astype(ref.dtype)


def down_sums(scalars, rows, down, capacity):
    units, feats = down.shape
    slots = rows.shape[0] // PAD * capacity
    part = slots // NX
    return pl.pallas_call(
        lambda *refs: down_kernel(capacity, *refs),
        in_specs=[SM, VM, VM],
        out_specs=[VM] * 4,
        out_shape=[jax.ShapeDtypeStruct((part, units), F32)]
        + [jax.ShapeDtypeStruct((part, units), BF)] * 3,
        scratch_shapes=[pltpu.VMEM((slots, units), F32)],
        cost_estimate=pl.CostEstimate(
            flops=2 * slots * feats * units, bytes_accessed=4_000_000, transcendentals=0
        ),
        compiler_params=pltpu.CompilerParams(vmem_limit_bytes=VMEM_BYTES),
        name="down_sums",
    )(scalars, rows, down)


def unit_kernel(capacity, scalars, *refs):
    sums, pres = refs[:NX], refs[NX : 2 * NX]
    w_gate, w_up, out_ref, dgate, dupper, shares = refs[2 * NX :]
    part, units = sums[0].shape
    for d, ref, pre in zip((0,) + STEPS, sums, pres):
        rows = pl.ds(pl.multiple_of((scalars[3] + NX - d) % NX * part, 16), part)
        summed = ref[...].astype(F32)
        both = pre[...]
        gate = both[:, :units].astype(F32)
        upper = both[:, units:].astype(F32)
        sig = jax.nn.sigmoid(gate)
        inside = gate * sig
        shares[rows, :] = jnp.broadcast_to(
            jnp.sum(inside * upper * summed, axis=1, keepdims=True), (part, 128)
        )
        dgate[rows, :] = (summed * upper * sig * (1.0 + gate * (1.0 - sig))).astype(BF)
        dupper[rows, :] = (summed * inside).astype(BF)
    back = lax.dot_general(dgate[...], w_gate[...], NT, preferred_element_type=F32)
    back = (back + lax.dot_general(dupper[...], w_up[...], NT, preferred_element_type=F32)).astype(BF)
    count, slots = out_ref.shape[0], back.shape[0]
    row, slot = iotas(count, slots)
    spread = (slot // capacity * PAD + slot % capacity == row).astype(F32).astype(BF)
    out_ref[...] = jnp.dot(spread, back, preferred_element_type=F32).astype(BF)
    slot, lane = iotas(slots, 128)
    along = jnp.where(slot % capacity == lane, shares[...], 0.0).astype(BF)
    spare = (slot_of(row, capacity) == iotas(count, slots)[1] // capacity).astype(F32).astype(BF)
    out_ref[:, :128] = (
        out_ref[:, :128].astype(F32) + jnp.dot(spare, along, preferred_element_type=F32)
    ).astype(BF)


def slot_of(row, capacity):
    return jnp.where(row % PAD == capacity, row // PAD, -1)


def unit_grads(scalars, sums, pre, w_gate, w_up, capacity):
    part, units = sums[0].shape
    slots = part * NX
    feats = w_gate.shape[0]
    return pl.pallas_call(
        lambda *refs: unit_kernel(capacity, *refs),
        in_specs=[SM] + [VM] * (2 * NX + 2),
        out_specs=VM,
        out_shape=jax.ShapeDtypeStruct((slots // capacity * PAD, feats), BF),
        scratch_shapes=[
            pltpu.VMEM((slots, units), BF),
            pltpu.VMEM((slots, units), BF),
            pltpu.VMEM((slots, 128), F32),
        ],
        cost_estimate=pl.CostEstimate(
            flops=4 * slots * feats * units, bytes_accessed=7_000_000, transcendentals=slots * units
        ),
        compiler_params=pltpu.CompilerParams(vmem_limit_bytes=VMEM_BYTES),
        name="unit_grads",
    )(scalars, *sums, *pre, w_gate, w_up)


def combine_kernel(
    capacity, back_ref, taken, chosen, gate, grad, others, scatter, routes, out_ref, gates_ref
):
    rows = back_ref[...].astype(F32) * gate[...]
    high = rows.astype(BF)
    low = (rows - high.astype(F32)).astype(BF)
    added = jnp.dot(taken[...], high, preferred_element_type=F32) + jnp.dot(
        taken[...], low, preferred_element_type=F32
    )
    lead = (grad[...] + added).astype(BF)
    placed = jnp.dot(scatter[...], lead, preferred_element_type=F32)
    out_ref[...] = (others[...].astype(F32) + placed).astype(BF)
    count = back_ref.shape[0]
    row, source = iotas(count, count)
    spare = (row // PAD * PAD + capacity == source).astype(F32).astype(BF)
    along = jnp.dot(spare, back_ref[:, :128], preferred_element_type=F32)
    row, lane = iotas(count, 128)
    share = jnp.sum(jnp.where(row % PAD == lane, along, 0.0), axis=1, keepdims=True)
    held = chosen[...].astype(F32) * share
    row, _ = iotas(count, held.shape[1])
    for k in range(2):
        named = row // PAD == routes[k : k + 1, :]
        gates_ref[k : k + 1, :] = jnp.sum(jnp.where(named, held, 0.0), axis=0, keepdims=True)


def combine(back, taken, chosen, gate, grad, others, scatter, routes, capacity):
    tokens, feats = others.shape
    return pl.pallas_call(
        lambda *refs: combine_kernel(capacity, *refs),
        in_specs=[VM] * 8,
        out_specs=[VM, VM],
        out_shape=[
            jax.ShapeDtypeStruct((tokens, feats), BF),
            jax.ShapeDtypeStruct((2, tokens), F32),
        ],
        cost_estimate=pl.CostEstimate(
            flops=2 * tokens * feats * 1024, bytes_accessed=8_000_000, transcendentals=0
        ),
        compiler_params=pltpu.CompilerParams(vmem_limit_bytes=VMEM_BYTES),
        name="combine_rows",
    )(back, taken, chosen, gate, grad, others, scatter, routes)


def dot_nt(left, right):
    return lax.dot_general(left, right, NT, preferred_element_type=F32)


def sum_x(mine, parts):
    moved = [expert_move(p, d, 0).astype(F32) for p, d in zip(parts, STEPS)]
    return ((mine + moved[0]) + (moved[1] + moved[2])).astype(BF)


def sum_z(mine):
    return (mine.astype(F32) + expert_move(mine, 0, 1).astype(F32)).astype(BF)


def all_x(mine):
    return [mine] + [expert_move(mine, d, 0) for d in STEPS]


def gather_x(block):
    return lax.all_gather(block, "expert", axis=0, axis_index_groups=X_GROUPS)


def after(value, *others):
    return lax.optimization_barrier((value,) + others)[0]


def per_device(
    hidden,
    routes,
    gates,
    saved_pre,
    w_gate,
    w_up,
    w_down,
    mtp_proj,
    mtp_gain,
    mtp_cotangent,
    main_cotangent,
):
    tokens, feats = hidden.shape
    experts = lax.axis_size("dp")
    slots = saved_pre.shape[1] * NE
    capacity = slots // experts
    lead = (slots + 127) // 128 * 128
    dp, ex = lax.axis_index("dp"), lax.axis_index("expert")
    x, h = ex // NZH, ex % NZH
    scalars = jnp.stack(
        [dp // (NZ * NC), (dp // NC) % NZ, dp % NC, x, h, x, x, x]
        + [i * NZH + (h + o) % NZH for o in range(NZH) for i in range(NX)]
    ).astype(jnp.int32)
    gain = mtp_gain[None, :]

    stack = line_z(mtp_proj.T)
    proj = gather_proj(stack)

    by_route = routes.T
    ids = jnp.arange(experts, dtype=jnp.int32)[:, None]
    first, second = by_route[0:1] == ids, by_route[1:2] == ids
    named = first | second
    routed = jnp.any(named, axis=0, keepdims=True)
    marks = jnp.concatenate([named, routed], axis=0).astype(BF)
    earlier = (
        lax.broadcasted_iota(jnp.int32, (tokens, tokens), 0)
        < lax.broadcasted_iota(jnp.int32, (tokens, tokens), 1)
    ).astype(BF)
    ranks = jnp.dot(marks, earlier, preferred_element_type=F32)
    number = jnp.sum(routed.astype(jnp.int32))
    ahead = ranks[experts].astype(jnp.int32)
    token = jnp.arange(tokens, dtype=jnp.int32)
    place = jnp.where(routed[0], ahead, number + token - ahead)
    order = (token[:, None] == place[None, :]).astype(BF)
    order_lead = (token[:lead, None] == place[None, :]).astype(BF)
    order_rest = (token[lead:, None] == place[None, :]).astype(BF)

    turned = mtp_cotangent.T
    cot_lead = after(dot_nt(turned, order_lead).astype(BF), stack)
    cot_rest = dot_nt(turned, order_rest).astype(BF)
    own_lead = gather_x(cot_lead)
    lead_swap = expert_move(cot_lead, 0, 1)
    hid = jnp.dot(order, hidden, preferred_element_type=F32).astype(BF)
    main = jnp.dot(order, main_cotangent, preferred_element_type=F32).astype(BF)
    far_lead = gather_x(after(lead_swap, own_lead, hid, main, proj[1][0], proj[2][0]))
    one = expert_move(after(cot_rest[:, :lead], lead_swap), 0, 1)
    two = expert_move(after(cot_rest[:, lead:], one), 0, 1)
    rest_swap = jnp.concatenate([one, two], axis=1)
    pre_own = saved_pre[0]
    pre_swap = expert_move(after(pre_own, lead_swap), 0, 1)
    pre_pair = jnp.concatenate(
        [jnp.where(h == 0, pre_own, pre_swap), jnp.where(h == 0, pre_swap, pre_own)], axis=0
    )
    near = gather_x(after(cot_rest, far_lead, one, pre_pair, *[a for a, _ in proj]))
    rows = experts * PAD
    seat = jnp.where(named, ranks[:experts] + 1.0, 0.0).astype(BF)
    row = lax.broadcasted_iota(jnp.int32, (rows, experts), 0)
    spread = (row // PAD == lax.broadcasted_iota(jnp.int32, (rows, experts), 1)).astype(BF)
    want = (jnp.arange(rows, dtype=jnp.int32) % PAD + 1).astype(F32)
    taken = jnp.dot(spread, seat, preferred_element_type=F32) == want[:, None]
    chosen = taken.astype(BF)
    gate = jnp.where(first, gates[:, 0][None, :], jnp.where(second, gates[:, 1][None, :], 0.0))
    gate = jnp.broadcast_to(gate[:, None], (experts, PAD, tokens)).reshape(rows, tokens)
    slot_gate = jnp.sum(jnp.where(taken, gate, 0.0), axis=1, keepdims=True)
    chosen_lead = dot_nt(chosen, order_lead).astype(BF)
    taken_lead = dot_nt(order_lead, chosen).astype(BF)
    order_back = (place[:, None] == token[None, :lead]).astype(BF)

    hid_f = hid.astype(F32)
    squares = jnp.sum(hid_f * hid_f, axis=1)
    ng_lead, inner = first_grads(scalars, proj, (own_lead, far_lead), hid, gain)
    both = jnp.concatenate([inner[:, 0], squares]).reshape(8, -1)
    both = expert_sum(both).reshape(-1)
    inner, squares = both[:lead], both[lead:]
    inverse = lax.rsqrt(squares / D + EPS)
    pull = inverse[:lead] ** 3 * inner / D
    grad_lead, outgoing = dispatch(
        ng_lead, hid, main, gain, inverse[:lead, None], pull[:, None], chosen_lead
    )
    far = gather_x(after(rest_swap, near, outgoing))
    pre = all_x(after(pre_pair, outgoing))
    arrived = lax.all_to_all(
        outgoing.reshape(experts, PAD, feats), "dp", split_axis=0, concat_axis=0, tiled=True
    ).reshape(rows, feats)

    normed = (hid.astype(F32) * inverse[:, None] * gain).astype(BF)
    mine, *parts = down_sums(after(scalars, *pre), arrived, w_down[0], capacity)
    mine = sum_x(mine, parts)
    own, other = proj_partials(after(scalars, mine), own_lead, near, far_lead, far, normed)
    mine = sum_z(mine)
    by_y = over_y(chip_sums(own, other, mine))
    back = unit_grads(scalars, all_x(mine), pre, w_gate[0], w_up[0], capacity)
    ng_rest, inner_rest = rest_grads(after(scalars, back), proj, near, far, hid, gain)
    inner_rest = expert_sum(inner_rest[:, 0].reshape(8, -1)).reshape(tokens - lead)
    grad_proj = over_z(by_y)
    returned = lax.all_to_all(
        back.reshape(experts, PAD, feats), "dp", split_axis=0, concat_axis=0, tiled=True
    ).reshape(rows, feats)

    late = after(inverse[lead:], grad_proj)
    grad_rest = (
        main[lead:].astype(F32)
        + late[:, None] * gain * ng_rest
        - hid[lead:].astype(F32) * (late**3 * inner_rest / D)[:, None]
    ).astype(BF)
    others = lax.dot_general(order_rest, grad_rest, TN, preferred_element_type=F32).astype(BF)
    grad_input, gate_rows = combine(
        after(returned, by_y), taken_lead, chosen, slot_gate, grad_lead, others, order_back, by_route, capacity
    )
    return (grad_input, gate_rows.T.astype(BF), grad_proj)


def solution(mesh):
    return jax.shard_map(
        per_device,
        mesh=mesh,
        in_specs=(
            P("dp", "expert"),
            P("dp", None),
            P("dp", None),
            P("dp", "expert", None),
            P("dp", "expert", None),
            P("dp", "expert", None),
            P("dp", None, "expert"),
            P("expert", "dp"),
            P("expert"),
            P("dp", "expert"),
            P("dp", "expert"),
        ),
        out_specs=(P("dp", "expert"), P("dp", None), P("expert", "dp")),
        check_vma=False,
    )
```

```python
import jax
import jax.numpy as jnp
from jax import lax
from jax.experimental import pallas as pl
from jax.experimental.pallas import tpu as pltpu
from jax.sharding import PartitionSpec as P

D = 7168
EPS = 1e-06
NX, NZH = 4, 2
NY, NZ, NC = 4, 4, 2
NE = NX * NZH
ND = NY * NZ * NC
BF = jnp.bfloat16
F32 = jnp.float32
STEPS = (1, 3, 2)
Y_GROUPS = [
    [(y * NZ + z) * NC + c for y in range(NY)] for z in range(NZ) for c in range(NC)
]
X_GROUPS = [[x * NZH + h for x in range(NX)] for h in range(NZH)]
PAD = 16
HBM = pl.BlockSpec(memory_space=pltpu.HBM)
TN = (((0,), (0,)), ((), ()))
VM = pl.BlockSpec(memory_space=pltpu.VMEM)
SM = pl.BlockSpec(memory_space=pltpu.SMEM)
VMEM_BYTES = 54 * 2**20


def expert_move(value, dx, dz):
    pairs = [
        (x * NZH + h, ((x + dx) % NX) * NZH + (h + dz) % NZH) for x in range(NX) for h in range(NZH)
    ]
    return lax.ppermute(value, "expert", pairs)


def dp_move(value, dy, dz, dc):
    pairs = [
        ((y * NZ + z) * NC + c, (((y + dy) % NY) * NZ + (z + dz) % NZ) * NC + (c + dc) % NC)
        for y in range(NY)
        for z in range(NZ)
        for c in range(NC)
    ]
    return lax.ppermute(value, "dp", pairs)


def expert_sum(value):
    value = value + expert_move(value, 0, 1)
    return (value + expert_move(value, 1, 0)) + (expert_move(value, 2, 0) + expert_move(value, 3, 0))


def block_of(array, index):
    return lax.dynamic_index_in_dim(array, index, 0, keepdims=False)


def line_z(shard):
    return jnp.concatenate([shard] + [dp_move(shard, 0, d, 0) for d in STEPS], axis=0)


def gather_proj(stack):
    line = (0,) + STEPS
    half = stack.shape[0] // 2
    below, above = dp_move(stack, 1, 0, 0), dp_move(stack, NY - 1, 0, 0)
    two_below, two_above = dp_move(below[:half], 1, 0, 0), dp_move(above[half:], NY - 1, 0, 0)
    near = [
        (stack, [(0, e) for e in line]),
        (below, [(1, e) for e in line]),
        (above, [(NY - 1, e) for e in line]),
        (two_below, [(2, e) for e in line[:2]]),
        (two_above, [(2, e) for e in line[2:]]),
    ]
    return [
        (dp_move(a, 0, 0, 1) if c else a, [(d, e, c) for d, e in steps])
        for c in range(NC)
        for a, steps in near
    ]


def proj_copies(scalars, refs, layout, scratch, sems, size):
    y, z, c = scalars[0], scalars[1], scalars[2]
    copies = []
    for ref, steps in zip(refs, layout):
        for i, (dy, dz, dc) in enumerate(steps):
            at = ((y + NY - dy) % NY * NZ + (z + NZ - dz) % NZ) * NC + (c + dc) % NC
            row = pl.multiple_of(at * size, 16)
            copies.append(
                pltpu.make_async_copy(
                    ref.at[pl.ds(i * size, size)], scratch.at[pl.ds(row, size)], sems.at[len(copies)]
                )
            )
    return copies


def lead_copies(scalars, refs, scratch, sems):
    width, lead = scratch.shape[0] // NE, scratch.shape[1]
    copies = []
    for o, ref in enumerate(refs):
        for x in range(NX):
            row = pl.multiple_of((x * NZH + (scalars[4] + o) % NZH) * width, 64)
            copies.append(
                pltpu.make_async_copy(
                    ref.at[x, :, pl.ds(0, lead)], scratch.at[pl.ds(row, width)], sems.at[len(copies)]
                )
            )
    return copies


def first_kernel(layout, scalars, *refs):
    n = len(layout)
    proj_refs, cot_refs = refs[:n], refs[n : n + NZH]
    hidden_ref, gain_ref, ng_ref, inner_ref, proj, cot, proj_sems, cot_sems = refs[n + NZH :]
    size = proj.shape[0] // ND
    copies = proj_copies(scalars, proj_refs, layout, proj, proj_sems, size)
    copies += lead_copies(scalars, cot_refs, cot, cot_sems)
    for copy in copies:
        copy.start()
    for copy in copies:
        copy.wait()
    part = lax.dot_general(cot[...], proj[...], TN, preferred_element_type=F32)
    ng_ref[...] = part
    total = jnp.sum(hidden_ref[...].astype(F32) * gain_ref[...] * part, axis=1, keepdims=True)
    inner_ref[...] = jnp.broadcast_to(total, inner_ref.shape)


def first_grads(scalars, proj, cots, hidden, gain):
    _, width, rows = cots[1].shape
    feats = hidden.shape[1]
    layout = [steps for _, steps in proj]
    block = lambda *shape: pl.BlockSpec(shape, lambda i: (0, 0))
    return pl.pallas_call(
        lambda *refs: first_kernel(layout, *refs),
        grid=(1,),
        in_specs=[SM] + [HBM] * (len(proj) + NZH) + [block(rows, feats), block(1, feats)],
        out_specs=[block(rows, feats), block(rows, 128)],
        out_shape=[
            jax.ShapeDtypeStruct((rows, feats), F32),
            jax.ShapeDtypeStruct((rows, 128), F32),
        ],
        scratch_shapes=[
            pltpu.VMEM((NE * width, feats), BF),
            pltpu.VMEM((NE * width, rows), BF),
            pltpu.SemaphoreType.DMA((ND,)),
            pltpu.SemaphoreType.DMA((NE,)),
        ],
        cost_estimate=pl.CostEstimate(
            flops=2 * rows * feats * NE * width, bytes_accessed=12_000_000, transcendentals=0
        ),
        compiler_params=pltpu.CompilerParams(vmem_limit_bytes=VMEM_BYTES),
        name="first_grads",
    )(scalars, *[a for a, _ in proj], *cots, hidden, gain)


def rest_kernel(layout, scalars, *refs):
    n = len(layout)
    proj_refs = refs[:n]
    own_ref, far_ref, hidden_ref, gain_ref, ng_ref, inner_ref, proj, cot, proj_sems = refs[n:]
    width = own_ref.shape[1]

    @pl.when(pl.program_id(0) == 0)
    def _():
        copies = proj_copies(scalars, proj_refs, layout, proj, proj_sems, width // 4)
        for copy in copies:
            copy.start()
        for copy in copies:
            copy.wait()

    for x in range(NX):
        for ref, o in ((own_ref, 0), (far_ref, 1)):
            row = pl.multiple_of((x * NZH + (scalars[4] + o) % NZH) * width, 64)
            cot[pl.ds(row, width), :] = ref[x]
    part = lax.dot_general(cot[...], proj[...], TN, preferred_element_type=F32)
    ng_ref[...] = part
    late = hidden_ref[hidden_ref.shape[0] - part.shape[0] :, :].astype(F32)
    total = jnp.sum(late * gain_ref[...] * part, axis=1, keepdims=True)
    inner_ref[...] = jnp.broadcast_to(total, inner_ref.shape)


def rest_grads(scalars, proj, own, far, hidden, gain):
    _, width, rest = far.shape
    tokens, feats = hidden.shape
    tile = rest
    layout = [steps for _, steps in proj]
    return pl.pallas_call(
        lambda *refs: rest_kernel(layout, *refs),
        grid=(rest // tile,),
        in_specs=[SM]
        + [HBM] * len(proj)
        + [
            pl.BlockSpec((NX, width, tile), lambda i: (0, 0, i)),
            pl.BlockSpec((NX, width, tile), lambda i: (0, 0, i)),
            pl.BlockSpec((tokens, feats), lambda i: (0, 0)),
            pl.BlockSpec((1, feats), lambda i: (0, 0)),
        ],
        out_specs=[
            pl.BlockSpec((tile, feats), lambda i: (i, 0)),
            pl.BlockSpec((tile, 128), lambda i: (i, 0)),
        ],
        out_shape=[
            jax.ShapeDtypeStruct((rest, feats), F32),
            jax.ShapeDtypeStruct((rest, 128), F32),
        ],
        scratch_shapes=[
            pltpu.VMEM((NE * width, feats), BF),
            pltpu.VMEM((NE * width, tile), BF),
            pltpu.SemaphoreType.DMA((ND,)),
        ],
        cost_estimate=pl.CostEstimate(
            flops=2 * rest * feats * NE * width, bytes_accessed=16_000_000, transcendentals=0
        ),
        compiler_params=pltpu.CompilerParams(vmem_limit_bytes=VMEM_BYTES),
        name="rest_grads",
    )(scalars, *[a for a, _ in proj], own, far, hidden, gain)


def partial_kernel(scalars, *refs):
    lead_ref, near_ref, far_lead_ref, far_ref, normed_ref, own_ref, other_ref, cot = refs
    width = cot.shape[0]
    lead = lead_ref.shape[2]
    size = width // 4
    step = pl.program_id(0)

    @pl.when(step < NX)
    def _():
        cot[:, :lead] = lead_ref[0]
        cot[:, lead:] = near_ref[0]

    @pl.when(step >= NX)
    def _():
        cot[:, :lead] = far_lead_ref[0]
        cot[:, lead:] = far_ref[0]

    part = jnp.dot(cot[...], normed_ref[...], preferred_element_type=F32)
    first = scalars[2] == 0
    for z in range(2):
        zero = part[(2 * z) * size : (2 * z + 1) * size]
        one = part[(2 * z + 1) * size : (2 * z + 2) * size]
        own_ref[0, z] = jnp.where(first, zero, one)
        other_ref[0, z] = jnp.where(first, one, zero).astype(BF)


def proj_partials(scalars, lead, near, far_lead, far, normed):
    tokens, feats = normed.shape
    _, width, rest = near.shape
    size = width // 4
    early = lambda i, s: (jnp.minimum(i, NX - 1), 0, 0)
    later = lambda i, s: (jnp.maximum(i - NX, 0), 0, 0)
    placed = pl.BlockSpec((1, 2, size, feats), lambda i, s: (s[8 + i], 0, 0, 0))
    return pl.pallas_call(
        partial_kernel,
        grid_spec=pltpu.PrefetchScalarGridSpec(
            num_scalar_prefetch=1,
            grid=(NE,),
            in_specs=[
                pl.BlockSpec((1, width, tokens - rest), early),
                pl.BlockSpec((1, width, rest), early),
                pl.BlockSpec((1, width, tokens - rest), later),
                pl.BlockSpec((1, width, rest), later),
                pl.BlockSpec((tokens, feats), lambda i, s: (0, 0)),
            ],
            out_specs=[placed, placed],
            scratch_shapes=[pltpu.VMEM((width, tokens), BF)],
        ),
        out_shape=[
            jax.ShapeDtypeStruct((NE, 2, size, feats), F32),
            jax.ShapeDtypeStruct((NE, 2, size, feats), BF),
        ],
        cost_estimate=pl.CostEstimate(
            flops=2 * tokens * feats * NE * width, bytes_accessed=20_000_000, transcendentals=0
        ),
        compiler_params=pltpu.CompilerParams(vmem_limit_bytes=VMEM_BYTES),
        name="proj_partials",
    )(scalars, lead, near, far_lead, far, normed)


def chip_sums(own, other, sums):
    size, feats = own.shape[2:]
    other = dp_move(other, 0, 0, 1)
    chip = (after(own, sums) + other.astype(F32)).astype(BF)
    return chip.reshape(NY, NZ, size, feats)


def over_y(chip):
    flat = chip.reshape(-1, chip.shape[3])
    out = lax.psum_scatter(flat, "dp", axis_index_groups=Y_GROUPS, tiled=True)
    return out.reshape(chip.shape[1:])


def over_z(line):
    z = (lax.axis_index("dp") // NC) % NZ
    moved = [dp_move(block_of(line, (z + d) % NZ), 0, d, 0).astype(F32) for d in STEPS]
    return ((block_of(line, z).astype(F32) + moved[0]) + (moved[1] + moved[2])).T


NT = (((1,), (1,)), ((), ()))


def dispatch_kernel(ng, hidden, main, gain, scale, pull, chosen, grad_ref, out_ref):
    grad = (
        main[...].astype(F32)
        + scale[...] * gain[...] * ng[...]
        - hidden[...].astype(F32) * pull[...]
    )
    grad_ref[...] = grad
    out_ref[...] = jnp.dot(chosen[...], grad.astype(BF), preferred_element_type=F32).astype(BF)


def dispatch(ng, hidden, main, gain, scale, pull, chosen):
    lead, feats = ng.shape
    rows = chosen.shape[0]
    block = lambda *shape: pl.BlockSpec(shape, lambda i: (0, 0))
    return pl.pallas_call(
        dispatch_kernel,
        grid=(1,),
        in_specs=[
            block(lead, feats),
            block(lead, feats),
            block(lead, feats),
            block(1, feats),
            block(lead, 1),
            block(lead, 1),
            block(rows, lead),
        ],
        out_specs=[block(lead, feats), block(rows, feats)],
        out_shape=[
            jax.ShapeDtypeStruct((lead, feats), F32),
            jax.ShapeDtypeStruct((rows, feats), BF),
        ],
        cost_estimate=pl.CostEstimate(
            flops=2 * rows * lead * feats, bytes_accessed=5_000_000, transcendentals=0
        ),
        compiler_params=pltpu.CompilerParams(vmem_limit_bytes=VMEM_BYTES),
        name="dispatch_rows",
    )(ng, hidden, main, gain, scale, pull, chosen)


def iotas(rows, columns):
    return [lax.broadcasted_iota(jnp.int32, (rows, columns), d) for d in (0, 1)]


def down_kernel(capacity, scalars, rows_ref, down_ref, mine_ref, one_ref, three_ref, two_ref, total):
    slot, row = iotas(total.shape[0], rows_ref.shape[0])
    packed = (slot // capacity * PAD + slot % capacity == row).astype(F32).astype(BF)
    rows = jnp.dot(packed, rows_ref[...], preferred_element_type=F32).astype(BF)
    total[...] = lax.dot_general(rows, down_ref[...], NT, preferred_element_type=F32)
    part = mine_ref.shape[0]
    for d, ref in zip((0,) + STEPS, (mine_ref, one_ref, three_ref, two_ref)):
        at = pl.multiple_of((scalars[3] + d) % NX * part, 8)
        ref[...] = total[pl.ds(at, part), :].astype(ref.dtype)


def down_sums(scalars, rows, down, capacity):
    units, feats = down.shape
    slots = rows.shape[0] // PAD * capacity
    part = slots // NX
    return pl.pallas_call(
        lambda *refs: down_kernel(capacity, *refs),
        in_specs=[SM, VM, VM],
        out_specs=[VM] * 4,
        out_shape=[jax.ShapeDtypeStruct((part, units), F32)]
        + [jax.ShapeDtypeStruct((part, units), BF)] * 3,
        scratch_shapes=[pltpu.VMEM((slots, units), F32)],
        cost_estimate=pl.CostEstimate(
            flops=2 * slots * feats * units, bytes_accessed=4_000_000, transcendentals=0
        ),
        compiler_params=pltpu.CompilerParams(vmem_limit_bytes=VMEM_BYTES),
        name="down_sums",
    )(scalars, rows, down)


def unit_kernel(capacity, scalars, *refs):
    sums, pres = refs[:NX], refs[NX : 2 * NX]
    w_gate, w_up, out_ref, dgate, dupper, shares = refs[2 * NX :]
    part, units = sums[0].shape
    for d, ref, pre in zip((0,) + STEPS, sums, pres):
        rows = pl.ds(pl.multiple_of((scalars[3] + NX - d) % NX * part, 16), part)
        summed = ref[...].astype(F32)
        both = pre[...]
        gate = both[:, :units].astype(F32)
        upper = both[:, units:].astype(F32)
        sig = jax.nn.sigmoid(gate)
        inside = gate * sig
        shares[rows, :] = jnp.broadcast_to(
            jnp.sum(inside * upper * summed, axis=1, keepdims=True), (part, 128)
        )
        dgate[rows, :] = (summed * upper * sig * (1.0 + gate * (1.0 - sig))).astype(BF)
        dupper[rows, :] = (summed * inside).astype(BF)
    back = lax.dot_general(dgate[...], w_gate[...], NT, preferred_element_type=F32)
    back = (back + lax.dot_general(dupper[...], w_up[...], NT, preferred_element_type=F32)).astype(BF)
    count, slots = out_ref.shape[0], back.shape[0]
    row, slot = iotas(count, slots)
    spread = (slot // capacity * PAD + slot % capacity == row).astype(F32).astype(BF)
    out_ref[...] = jnp.dot(spread, back, preferred_element_type=F32).astype(BF)
    slot, lane = iotas(slots, 128)
    along = jnp.where(slot % capacity == lane, shares[...], 0.0).astype(BF)
    spare = (slot_of(row, capacity) == iotas(count, slots)[1] // capacity).astype(F32).astype(BF)
    out_ref[:, :128] = (
        out_ref[:, :128].astype(F32) + jnp.dot(spare, along, preferred_element_type=F32)
    ).astype(BF)


def slot_of(row, capacity):
    return jnp.where(row % PAD == capacity, row // PAD, -1)


def unit_grads(scalars, sums, pre, w_gate, w_up, capacity):
    part, units = sums[0].shape
    slots = part * NX
    feats = w_gate.shape[0]
    return pl.pallas_call(
        lambda *refs: unit_kernel(capacity, *refs),
        in_specs=[SM] + [VM] * (2 * NX + 2),
        out_specs=VM,
        out_shape=jax.ShapeDtypeStruct((slots // capacity * PAD, feats), BF),
        scratch_shapes=[
            pltpu.VMEM((slots, units), BF),
            pltpu.VMEM((slots, units), BF),
            pltpu.VMEM((slots, 128), F32),
        ],
        cost_estimate=pl.CostEstimate(
            flops=4 * slots * feats * units, bytes_accessed=7_000_000, transcendentals=slots * units
        ),
        compiler_params=pltpu.CompilerParams(vmem_limit_bytes=VMEM_BYTES),
        name="unit_grads",
    )(scalars, *sums, *pre, w_gate, w_up)


def combine_kernel(
    capacity, back_ref, taken, chosen, gate, grad, others, scatter, routes, out_ref, gates_ref
):
    rows = back_ref[...].astype(F32) * gate[...]
    high = rows.astype(BF)
    low = (rows - high.astype(F32)).astype(BF)
    added = jnp.dot(taken[...], high, preferred_element_type=F32) + jnp.dot(
        taken[...], low, preferred_element_type=F32
    )
    lead = (grad[...] + added).astype(BF)
    placed = jnp.dot(scatter[...], lead, preferred_element_type=F32)
    out_ref[...] = (others[...].astype(F32) + placed).astype(BF)
    count = back_ref.shape[0]
    row, source = iotas(count, count)
    spare = (row // PAD * PAD + capacity == source).astype(F32).astype(BF)
    along = jnp.dot(spare, back_ref[:, :128], preferred_element_type=F32)
    row, lane = iotas(count, 128)
    share = jnp.sum(jnp.where(row % PAD == lane, along, 0.0), axis=1, keepdims=True)
    held = chosen[...].astype(F32) * share
    row, _ = iotas(count, held.shape[1])
    for k in range(2):
        named = row // PAD == routes[k : k + 1, :]
        gates_ref[k : k + 1, :] = jnp.sum(jnp.where(named, held, 0.0), axis=0, keepdims=True)


def combine(back, taken, chosen, gate, grad, others, scatter, routes, capacity):
    tokens, feats = others.shape
    return pl.pallas_call(
        lambda *refs: combine_kernel(capacity, *refs),
        in_specs=[VM] * 8,
        out_specs=[VM, VM],
        out_shape=[
            jax.ShapeDtypeStruct((tokens, feats), BF),
            jax.ShapeDtypeStruct((2, tokens), F32),
        ],
        cost_estimate=pl.CostEstimate(
            flops=2 * tokens * feats * 1024, bytes_accessed=8_000_000, transcendentals=0
        ),
        compiler_params=pltpu.CompilerParams(vmem_limit_bytes=VMEM_BYTES),
        name="combine_rows",
    )(back, taken, chosen, gate, grad, others, scatter, routes)


def dot_nt(left, right):
    return lax.dot_general(left, right, NT, preferred_element_type=F32)


def sum_x(mine, parts):
    moved = [expert_move(p, d, 0).astype(F32) for p, d in zip(parts, STEPS)]
    return ((mine + moved[0]) + (moved[1] + moved[2])).astype(BF)


def sum_z(mine):
    return (mine.astype(F32) + expert_move(mine, 0, 1).astype(F32)).astype(BF)


def all_x(mine):
    return [mine] + [expert_move(mine, d, 0) for d in STEPS]


def gather_x(block):
    return lax.all_gather(block, "expert", axis=0, axis_index_groups=X_GROUPS)


def after(value, *others):
    return lax.optimization_barrier((value,) + others)[0]


def per_device(
    hidden,
    routes,
    gates,
    saved_pre,
    w_gate,
    w_up,
    w_down,
    mtp_proj,
    mtp_gain,
    mtp_cotangent,
    main_cotangent,
):
    tokens, feats = hidden.shape
    experts = lax.axis_size("dp")
    slots = saved_pre.shape[1] * NE
    capacity = slots // experts
    lead = (slots + 127) // 128 * 128
    dp, ex = lax.axis_index("dp"), lax.axis_index("expert")
    x, h = ex // NZH, ex % NZH
    scalars = jnp.stack(
        [dp // (NZ * NC), (dp // NC) % NZ, dp % NC, x, h, x, x, x]
        + [i * NZH + (h + o) % NZH for o in range(NZH) for i in range(NX)]
    ).astype(jnp.int32)
    gain = mtp_gain[None, :]

    stack = line_z(mtp_proj.T)
    proj = gather_proj(stack)

    by_route = routes.T
    ids = jnp.arange(experts, dtype=jnp.int32)[:, None]
    first, second = by_route[0:1] == ids, by_route[1:2] == ids
    named = first | second
    routed = jnp.any(named, axis=0, keepdims=True)
    marks = jnp.concatenate([named, routed], axis=0).astype(BF)
    earlier = (
        lax.broadcasted_iota(jnp.int32, (tokens, tokens), 0)
        < lax.broadcasted_iota(jnp.int32, (tokens, tokens), 1)
    ).astype(BF)
    ranks = jnp.dot(marks, earlier, preferred_element_type=F32)
    number = jnp.sum(routed.astype(jnp.int32))
    ahead = ranks[experts].astype(jnp.int32)
    token = jnp.arange(tokens, dtype=jnp.int32)
    place = jnp.where(routed[0], ahead, number + token - ahead)
    order = (token[:, None] == place[None, :]).astype(BF)
    order_lead = (token[:lead, None] == place[None, :]).astype(BF)
    order_rest = (token[lead:, None] == place[None, :]).astype(BF)

    turned = mtp_cotangent.T
    cot_lead = after(dot_nt(turned, order_lead).astype(BF), stack)
    cot_rest = dot_nt(turned, order_rest).astype(BF)
    own_lead = gather_x(cot_lead)
    lead_swap = expert_move(cot_lead, 0, 1)
    hid = jnp.dot(order, hidden, preferred_element_type=F32).astype(BF)
    main = jnp.dot(order, main_cotangent, preferred_element_type=F32).astype(BF)
    far_lead = gather_x(after(lead_swap, own_lead, hid, main, proj[1][0], proj[2][0]))
    one = expert_move(after(cot_rest[:, :lead], lead_swap), 0, 1)
    two = expert_move(after(cot_rest[:, lead:], one), 0, 1)
    rest_swap = jnp.concatenate([one, two], axis=1)
    pre_own = saved_pre[0]
    pre_swap = expert_move(after(pre_own, lead_swap), 0, 1)
    pre_pair = jnp.concatenate(
        [jnp.where(h == 0, pre_own, pre_swap), jnp.where(h == 0, pre_swap, pre_own)], axis=0
    )
    near = gather_x(after(cot_rest, far_lead, one, pre_pair, *[a for a, _ in proj]))
    rows = experts * PAD
    seat = jnp.where(named, ranks[:experts] + 1.0, 0.0).astype(BF)
    row = lax.broadcasted_iota(jnp.int32, (rows, experts), 0)
    spread = (row // PAD == lax.broadcasted_iota(jnp.int32, (rows, experts), 1)).astype(BF)
    want = (jnp.arange(rows, dtype=jnp.int32) % PAD + 1).astype(F32)
    taken = jnp.dot(spread, seat, preferred_element_type=F32) == want[:, None]
    chosen = taken.astype(BF)
    gate = jnp.where(first, gates[:, 0][None, :], jnp.where(second, gates[:, 1][None, :], 0.0))
    gate = jnp.broadcast_to(gate[:, None], (experts, PAD, tokens)).reshape(rows, tokens)
    slot_gate = jnp.sum(jnp.where(taken, gate, 0.0), axis=1, keepdims=True)
    chosen_lead = dot_nt(chosen, order_lead).astype(BF)
    taken_lead = dot_nt(order_lead, chosen).astype(BF)
    order_back = (place[:, None] == token[None, :lead]).astype(BF)

    hid_f = hid.astype(F32)
    squares = jnp.sum(hid_f * hid_f, axis=1)
    ng_lead, inner = first_grads(scalars, proj, (own_lead, far_lead), hid, gain)
    both = jnp.concatenate([inner[:, 0], squares]).reshape(8, -1)
    both = expert_sum(both).reshape(-1)
    inner, squares = both[:lead], both[lead:]
    inverse = lax.rsqrt(squares / D + EPS)
    pull = inverse[:lead] ** 3 * inner / D
    grad_lead, outgoing = dispatch(
        ng_lead, hid, main, gain, inverse[:lead, None], pull[:, None], chosen_lead
    )
    far = gather_x(after(rest_swap, near, outgoing))
    pre = all_x(after(pre_pair, outgoing))
    arrived = lax.all_to_all(
        outgoing.reshape(experts, PAD, feats), "dp", split_axis=0, concat_axis=0, tiled=True
    ).reshape(rows, feats)

    normed = (hid.astype(F32) * inverse[:, None] * gain).astype(BF)
    mine, *parts = down_sums(after(scalars, *pre), arrived, w_down[0], capacity)
    mine = sum_x(mine, parts)
    own, other = proj_partials(after(scalars, mine), own_lead, near, far_lead, far, normed)
    mine = sum_z(mine)
    by_y = over_y(chip_sums(own, other, mine))
    back = unit_grads(scalars, all_x(mine), pre, w_gate[0], w_up[0], capacity)
    ng_rest, inner_rest = rest_grads(after(scalars, back), proj, near, far, hid, gain)
    inner_rest = expert_sum(inner_rest[:, 0].reshape(8, -1)).reshape(tokens - lead)
    grad_proj = over_z(by_y)
    returned = lax.all_to_all(
        back.reshape(experts, PAD, feats), "dp", split_axis=0, concat_axis=0, tiled=True
    ).reshape(rows, feats)

    late = after(inverse[lead:], grad_proj)
    grad_rest = (
        main[lead:].astype(F32)
        + late[:, None] * gain * ng_rest
        - hid[lead:].astype(F32) * (late**3 * inner_rest / D)[:, None]
    ).astype(BF)
    others = lax.dot_general(order_rest, grad_rest, TN, preferred_element_type=F32).astype(BF)
    grad_input, gate_rows = combine(
        after(returned, by_y), taken_lead, chosen, slot_gate, grad_lead, others, order_back, by_route, capacity
    )
    return (grad_input, gate_rows.T.astype(BF), grad_proj)


def solution(mesh):
    return jax.shard_map(
        per_device,
        mesh=mesh,
        in_specs=(
            P("dp", "expert"),
            P("dp", None),
            P("dp", None),
            P("dp", "expert", None),
            P("dp", "expert", None),
            P("dp", "expert", None),
            P("dp", None, "expert"),
            P("expert", "dp"),
            P("expert"),
            P("dp", "expert"),
            P("dp", "expert"),
        ),
        out_specs=(P("dp", "expert"), P("dp", None), P("expert", "dp")),
        check_vma=False,
    )
```
